256 devices in a mesh: grp: 2 (over core), row: 16 (over y, x), col: 8 (over z).
Axes of the slice: x: 4, y: 4, z: 8, core: 2. Of those that a mesh axis runs over, the one named last changes fastest.
Arguments:
- raw_samples: bfloat16 [2, 8192, 2048], P(None, ('grp', 'row', 'col')), may hold values from -6 to 6
- window: float32 [2048], replicated, may hold values from 0.25 to 1.75
- steering: bfloat16 [8192, 2, 128], P(('grp', 'row', 'col')), may hold values from -0.375 to 0.375
- assignment: int32 [8192, 1], P(('grp', 'row', 'col')), may hold values from 0 to 15; in each aligned block of 32 rows (0 to 31, 32 to 63, ...) at most 6 rows name the same one
- beam_map: int32 [2, 2, 16, 2, 128], P(None, 'grp', 'row'), may hold values from 0 to 63
- interp_index: int32 [2, 2, 16, 2, 128], P(None, 'grp', 'row'), may hold values from 0 to 7
- phase_offset: float32 [2, 2, 16, 2, 128], P(None, 'grp', 'row'), may hold values from -3.140625 to 3.140625
- phase_rate: float32 [2, 2, 16, 2, 128], P(None, 'grp', 'row'), may hold values from -6 to 6
- interp_bank: bfloat16 [8, 128, 128], replicated, may hold values from -2 to 2
Outputs:
- image: bfloat16 [2, 16, 128, 2, 2048], P('grp', 'row', None, None, 'col')
The draws below stay inside these ranges and needn't reach their ends.
Inputs may be any that keep to these rules, and one draw needn't show every extreme that they name: `assignment`: each pulse names an owner along row within its own half of grp; on every device at most 6 pulses name one owner, and on some device exactly 6 do.
All inputs are finite; a program needn't handle non-finite values.
Results may differ from the reference program's by a relative error of at most 0.007.
Values may be sent and summed in bfloat16 or wider, within the bound.
A program may use at most 64 MiB of HBM per device.

```python
import math
import jax
import jax.numpy as jnp
import numpy as np
from jax import lax

NS = 2048
BEAMS = 128
RT = 128
Q = 8
LEVELS = 2
P_DEV = 32
CAP = 6
PULSES = 8192
N_GRP = 2
N_ROW = 16
N_COL = 8


def draw_interp_bank(key, part):
    key = jax.random.fold_in(key, 11)
    off_key, diag_key = jax.random.split(key)
    spread = jnp.clip(jax.random.normal(off_key, (Q, RT, RT), jnp.float32), -4.0, 4.0) * (0.5 / RT ** 0.5)
    diagonal = jax.random.uniform(diag_key, (Q, RT), jnp.float32, 0.7, 1.3)
    identity = jnp.eye(RT, dtype=jnp.float32)
    return (spread + diagonal[:, :, None] * identity[None]).astype(jnp.bfloat16)


def with_ends(drawn, own_key, least, largest):
    longest = drawn.shape.index(max(drawn.shape))
    spots = []
    for shift in (0, 1):
        where = [jax.random.randint(jax.random.fold_in(own_key, axis), (), 0, length) for axis, length in enumerate(drawn.shape)]
        where[longest] = (where[longest] + shift) % drawn.shape[longest]
        spots.append(tuple(where))
    return drawn.at[spots[0]].set(least).at[spots[1]].set(largest)


def shard_levels(rng, shape, cuts, least, top_value):
    level, own = 1.0, jax.random.fold_in(rng, 6)
    for dim, shards_of in cuts:
        heights = jnp.exp(jax.random.uniform(jax.random.fold_in(own, dim), (shards_of,), jnp.float32, least / len(cuts), top_value / len(cuts)))
        level = level * jnp.repeat(heights, shape[dim] // shards_of).reshape([-1 if axis == dim else 1 for axis in range(len(shape))])
    return level


def routed_block(own_key, own, number, rows, number_of, top, bound, slope):
    ranking = jax.random.permutation(own_key, number_of)
    packed, ordinary = shares(number_of, rows * top, bound, slope, True), shares(number_of, rows * top, bound, slope, False)
    places = jnp.arange(number_of)

    def named(sizes, turn):
        used = int((sizes > 0).sum())
        fixed = max(1, used // 4)
        shifted = fixed + (places - fixed + turn * (used - fixed)) % max(1, number_of - fixed)
        return jnp.zeros((number_of,), jnp.int32).at[ranking[jnp.where(places < fixed, places, shifted)]].set(jnp.asarray(sizes, jnp.int32))

    sizes = jnp.where(number % 4 == 0, named(packed, number // 4), named(ordinary, number - number // 4 - 1))
    mixed = jax.random.permutation(jax.random.fold_in(own, 3), number_of)
    source_of, taker = mixed[0:number_of // 2 * 2:2], mixed[1:number_of // 2 * 2:2]
    room = jnp.minimum(sizes[source_of] - 1, bound - sizes[taker]) // 2
    room = jnp.where((source_of == ranking[0]) | (taker == ranking[0]) | (sizes[taker] == 0), 0, jnp.maximum(room, 0))
    shifted = jax.random.randint(jax.random.fold_in(own, 4), (number_of // 2,), 0, 1 << 20) % (room + 1)
    sizes = sizes.at[source_of].add(-shifted).at[taker].add(shifted)
    labels = jnp.searchsorted(jnp.cumsum(sizes), jnp.arange(rows * top), side="right").astype(jnp.int32)
    table = labels.reshape(top, rows).T
    table = table[jax.random.permutation(jax.random.fold_in(own, 1), rows)]
    turn = jax.random.randint(jax.random.fold_in(own, 2), (rows, 1), 0, top)
    return jnp.take_along_axis(table, (jnp.arange(top)[None, :] + turn) % top, axis=1)


def shares(number_of, total, reach, skew, full):
    loads = [(1 << 20) // math.isqrt(standing ** skew) + 1 for standing in range(1, number_of + 1)]
    largest = reach if full else min(reach, max(-(-total // number_of), total * loads[0] // sum(loads)))
    least = 1 if total - largest >= number_of - 1 else 0
    given, rest = [largest] + [least] * (number_of - 1), total - largest - least * (number_of - 1)
    while rest > 0:
        candidates = [i for i in range(1, number_of) if given[i] < largest] or [i for i in range(1, number_of) if given[i] < reach]
        mass, left = sum([loads[i] for i in candidates]), rest
        for i in candidates:
            addition = min(reach - given[i], max(1, left * loads[i] // mass), rest)
            given[i] = given[i] + addition
            rest = rest - addition
    return np.array(given)


def bell_draw(stream_key, dims, width, reach, cuts=(), kind=jnp.bfloat16):
    entries = jax.random.normal(stream_key, dims, jnp.float32) * width
    if len(cuts) > 0:
        entries = shard_levels(stream_key, dims, cuts, -0.22, 0.18) * entries
    return jnp.clip(entries, min=-reach, max=reach).astype(kind)


def setup_inputs(seed: int = 0) -> dict:
    seeds = jax.random.split(jax.random.key(seed), 10)
    raw_samples = bell_draw(seeds[0], (2, PULSES, NS), 1.0, 6.0, ((1, 256),))
    window = jnp.clip(1.0 + 0.15 * jax.random.normal(seeds[1], (NS,), jnp.float32), 0.25, 1.75)
    steering = bell_draw(seeds[2], (PULSES, 2, BEAMS), (P_DEV * N_COL) ** -0.5, 0.375, ((0, 256),))
    assignment_keys = jax.random.split(jax.random.fold_in(seeds[3], 1), PULSES // P_DEV)
    assignment_turns = jax.random.permutation(jax.random.fold_in(seeds[3], 3), PULSES // P_DEV)
    assignment = jax.vmap(lambda own, number: routed_block(jax.random.fold_in(seeds[3], 2), own, number, P_DEV, N_ROW, 1, CAP, 2))(assignment_keys, assignment_turns).reshape((PULSES, 1))
    beam_map = with_ends(jax.random.randint(seeds[4], (LEVELS, N_GRP, N_ROW, 2, BEAMS), 0, BEAMS // 2), jax.random.fold_in(seeds[4], 1), 0, (BEAMS // 2) - 1).astype(jnp.int32)
    interp_index = with_ends(jax.random.randint(seeds[5], (LEVELS, N_GRP, N_ROW, 2, BEAMS), 0, Q), jax.random.fold_in(seeds[5], 1), 0, Q - 1).astype(jnp.int32)
    phase_offset = jnp.clip(jax.random.uniform(seeds[6], (LEVELS, N_GRP, N_ROW, 2, BEAMS), jnp.float32, -3.140625, 3.140625), -3.140625, 3.140625)
    phase_rate = jnp.clip(jax.random.uniform(seeds[7], (LEVELS, N_GRP, N_ROW, 2, BEAMS), jnp.float32, -6.0, 6.0) * shard_levels(seeds[7], (LEVELS, N_GRP, N_ROW, 2, BEAMS), ((1, 2), (2, 16)), -0.4, 0.0), -6.0, 6.0)
    interp_bank = draw_interp_bank(jax.random.fold_in(seeds[9], 71), 0)
    return dict(raw_samples=raw_samples, window=window, steering=steering, assignment=assignment, beam_map=beam_map, interp_index=interp_index, phase_offset=phase_offset, phase_rate=phase_rate, interp_bank=interp_bank)


def spectral_tables(window):
    sample = jnp.arange(NS, dtype=jnp.int32)
    phase_index = sample[:, None] * sample[None, :] % NS
    phase_angle = phase_index.astype(jnp.float32) * (2.0 * math.pi / NS)
    scaling = window[:, None] / math.sqrt(NS)
    cos_table = (jnp.cos(phase_angle) * scaling).astype(jnp.bfloat16)
    sin_table = (jnp.sin(phase_angle) * scaling).astype(jnp.bfloat16)
    return (cos_table, sin_table)

def interpolate(picked_rows, quants, offsets, rates, bank, positions):
    beam_count = picked_rows.shape[0]
    range_bins = picked_rows.shape[2]
    blocks = picked_rows.reshape(beam_count, 2, range_bins // RT, RT).astype(jnp.float32)
    all_phases = jnp.einsum('bctw,qwu->bctqu', blocks, bank.astype(jnp.float32))
    chosen = all_phases[:, :, :, 0]
    for bank_index in range(1, Q):
        chosen = jnp.where((quants == bank_index)[:, None, None, None], all_phases[:, :, :, bank_index], chosen)
    chosen = chosen.reshape(beam_count, 2, range_bins)
    phase_angle = offsets[:, None] + rates[:, None] * (positions[None, :] / NS)
    cosine = jnp.cos(phase_angle)
    sine_part = jnp.sin(phase_angle)
    real_part = chosen[:, 0] * cosine - chosen[:, 1] * sine_part
    imag_part = chosen[:, 0] * sine_part + chosen[:, 1] * cosine
    return jnp.stack([real_part, imag_part], axis=1)

def reference(raw_samples, window, steering, assignment, beam_map, interp_index, phase_offset, phase_rate, interp_bank):
    cos_table, sin_table = spectral_tables(window)
    block_size = P_DEV * 8
    block_count = PULSES // block_size

    def compress_block(pulse_block):
        real_in = pulse_block[0]
        imag_in = pulse_block[1]
        real_out = jnp.dot(real_in, cos_table, preferred_element_type=jnp.float32) + jnp.dot(imag_in, sin_table, preferred_element_type=jnp.float32)
        imag_out = jnp.dot(imag_in, cos_table, preferred_element_type=jnp.float32) - jnp.dot(real_in, sin_table, preferred_element_type=jnp.float32)
        return jnp.stack([real_out, imag_out], axis=1).astype(jnp.bfloat16)
    blocked = jnp.moveaxis(raw_samples.reshape(2, block_count, block_size, NS), 1, 0)
    compressed = lax.map(compress_block, blocked).reshape(PULSES, 2, NS)
    owner = assignment[:, 0]
    group_index = jnp.arange(PULSES, dtype=jnp.int32) // (PULSES // N_GRP)
    sort_key = group_index * N_ROW + owner
    order = jnp.argsort(sort_key, stable=True).astype(jnp.int32)
    counts = lax.optimization_barrier(jnp.sum((sort_key[:, None] == jnp.arange(N_GRP * N_ROW, dtype=jnp.int32)[None, :]).astype(jnp.int32), axis=0))
    starts = jnp.cumsum(counts) - counts
    slot_total = N_ROW * N_COL * CAP
    order_padded = jnp.concatenate([order, jnp.zeros((slot_total,), jnp.int32)])

    def level_zero(subaperture):
        start = starts[subaperture].astype(jnp.int32)
        picked = lax.dynamic_slice(order_padded, (start,), (slot_total,))
        valid = (jnp.arange(slot_total, dtype=jnp.int32) < counts[subaperture]).astype(jnp.bfloat16)
        weights = steering[picked] * valid[:, None, None]
        samples = compressed[picked]
        partial_value = jnp.einsum('sab,scr->abcr', weights.astype(jnp.float32), samples.astype(jnp.float32))
        real_part = partial_value[0, :, 0] - partial_value[1, :, 1]
        imag_part = partial_value[0, :, 1] + partial_value[1, :, 0]
        return jnp.stack([real_part, imag_part], axis=1).astype(jnp.bfloat16)
    image0 = lax.map(level_zero, jnp.arange(N_GRP * N_ROW, dtype=jnp.int32))
    image0 = image0.reshape(N_GRP, N_ROW, BEAMS, 2, NS)
    positions = jnp.arange(NS, dtype=jnp.float32)
    half_beams = BEAMS // 2

    def merge_device(operands):
        low_child, high_child, bit_value, maps, quants, offsets, rates = operands
        running_total = jnp.zeros((BEAMS, 2, NS), jnp.float32)
        for source, child_image in enumerate((low_child, high_child)):
            picked_rows = jnp.take(child_image, bit_value * half_beams + maps[source], axis=0)
            running_total = running_total + interpolate(picked_rows, quants[source], offsets[source], rates[source], interp_bank, positions)
        return running_total.astype(jnp.bfloat16)

    def level_args(level_index):
        shape_flat = (N_GRP * N_ROW, 2, BEAMS)
        return (beam_map[level_index].reshape(shape_flat), interp_index[level_index].reshape(shape_flat), phase_offset[level_index].reshape(shape_flat), phase_rate[level_index].reshape(shape_flat))
    flat_shape = (N_GRP * N_ROW, BEAMS, 2, NS)
    low_first = jnp.broadcast_to(image0[0][None], image0.shape).reshape(flat_shape)
    high_first = jnp.broadcast_to(image0[1][None], image0.shape).reshape(flat_shape)
    bits_first = jnp.repeat(jnp.arange(N_GRP, dtype=jnp.int32), N_ROW)
    image1 = lax.map(merge_device, (low_first, high_first, bits_first) + level_args(0))
    image1 = image1.reshape(N_GRP, N_ROW, BEAMS, 2, NS)
    pairs = image1.reshape(N_GRP, N_ROW // 2, 2, BEAMS, 2, NS)
    low_second = jnp.repeat(pairs[:, :, 0], 2, axis=1).reshape(flat_shape)
    high_second = jnp.repeat(pairs[:, :, 1], 2, axis=1).reshape(flat_shape)
    bits_second = jnp.tile(jnp.arange(N_ROW, dtype=jnp.int32) % 2, N_GRP)
    image = lax.map(merge_device, (low_second, high_second, bits_second) + level_args(1))
    return image.reshape(N_GRP, N_ROW, BEAMS, 2, NS)
```

```python
import math

import jax
import jax.numpy as jnp
from jax import lax
from jax.experimental import pallas as pl
from jax.experimental.pallas import tpu as pltpu
from jax.sharding import PartitionSpec as P

MESH = pl.DeviceIdType.MESH
F32, BF16, I32 = jnp.float32, jnp.bfloat16, jnp.int32

NS = 2048
BEAMS = 128
RT = 128
Q = 8
P_DEV = 32
CAP = 6
ROWS = 16
COLS = 8
SLOTS = COLS * CAP
HALF = BEAMS // 2
CHUNKS = 2

COS = (
    0.9999999890590227,
    -19.73920449945391,
    64.93911745989556,
    -85.45013953088247,
    60.16763095094928,
    -25.967599248494622,
    6.528658161366808,
)
SIN = (
    6.283185302511503,
    -41.341700405317496,
    81.60513138579344,
    -76.70301535379849,
    42.025926985567956,
    -14.89984666736486,
    3.238137509743233,
)


def horner(coefs, y):
    total = jnp.full_like(y, coefs[-1])
    for c in coefs[-2::-1]:
        total = total * y + c
    return total


def cos_sin(turns):
    r = turns - jnp.floor(turns + 0.5)
    y = r * r
    return horner(COS, y), horner(SIN, y) * r


def dft8(xr, xi):
    h = math.sqrt(0.5)
    ur = [xr[j] + xr[j + 4] for j in range(4)]
    ui = [xi[j] + xi[j + 4] for j in range(4)]
    vr = [xr[j] - xr[j + 4] for j in range(4)]
    vi = [xi[j] - xi[j + 4] for j in range(4)]
    wr = [vr[0], (vr[1] + vi[1]) * h, vi[2], (vi[3] - vr[3]) * h]
    wi = [vi[0], (vi[1] - vr[1]) * h, -vr[2], (-vr[3] - vi[3]) * h]
    yr, yi = [None] * 8, [None] * 8
    for odd, (zr, zi) in enumerate(((ur, ui), (wr, wi))):
        ar, ai = zr[0] + zr[2], zi[0] + zi[2]
        br, bi = zr[0] - zr[2], zi[0] - zi[2]
        cr, ci = zr[1] + zr[3], zi[1] + zi[3]
        dr, di = zr[1] - zr[3], zi[1] - zi[3]
        yr[odd], yi[odd] = ar + cr, ai + ci
        yr[odd + 4], yi[odd + 4] = ar - cr, ai - ci
        yr[odd + 2], yi[odd + 2] = br + di, bi - dr
        yr[odd + 6], yi[odd + 6] = br - di, bi + dr
    return yr, yi


def swap_groups(tiles):
    group = lax.broadcasted_iota(I32, tiles[0].shape, 1) // 16
    tiles = list(tiles)
    for bit in range(3):
        step = 1 << bit
        upper = (group // step) % 2 == 1
        for a in range(8):
            if a & step:
                continue
            low, high = tiles[a], tiles[a + step]
            tiles[a] = jnp.where(upper, pltpu.roll(high, 16 * step, 1), low)
            tiles[a + step] = jnp.where(upper, high, pltpu.roll(low, 128 - 16 * step, 1))
    return tiles


def dot(a, b):
    return jnp.dot(a, b, preferred_element_type=F32)


def iota(shape, dim):
    return lax.broadcasted_iota(I32, shape, dim)


def kernel(
    raw,
    window,
    steering,
    assignment,
    beam_map,
    interp_index,
    phase_offset,
    phase_rate,
    bank,
    out,
    ybuf,
    table,
    twiddle,
    st_own,
    st_all,
    code_own,
    code_all,
    dsend,
    zall,
    sel,
    slots,
    got,
    weights_t,
    par,
    bank_nat,
    bank_perm,
    picks,
    cosb,
    sinb,
    img,
    child,
    vbuf,
    outf,
    st_send,
    st_recv,
    code_send,
    code_recv,
    z_send,
    z_recv,
    r_send,
    r_recv,
    x_send,
    x_recv,
):
    g, row, col = lax.axis_index("grp"), lax.axis_index("row"), lax.axis_index("col")
    ry, rx = row // 4, row % 4

    def remote(src, dst, ssem, rsem, device):
        return pltpu.make_async_remote_copy(
            src_ref=src,
            dst_ref=dst,
            send_sem=ssem,
            recv_sem=rsem,
            device_id=device,
            device_id_type=MESH,
        )

    barrier = pltpu.get_barrier_semaphore()

    def greet_col(i, _):
        pl.semaphore_signal(
            barrier, inc=1, device_id=(g, row, (col + i) % COLS), device_id_type=MESH
        )
        return 0

    def greet_row(i, _):
        pl.semaphore_signal(
            barrier, inc=1, device_id=(g, (row + i) % ROWS, col), device_id_type=MESH
        )
        return 0

    lax.fori_loop(1, COLS, greet_col, 0)
    lax.fori_loop(1, ROWS, greet_row, 0)
    pl.semaphore_signal(barrier, inc=1, device_id=(1 - g, row, col), device_id_type=MESH)

    own_row = assignment[...].astype(F32)
    eye = iota((P_DEV, P_DEV), 0) == iota((P_DEV, P_DEV), 1)
    before = iota((P_DEV, P_DEV), 1) < iota((P_DEV, P_DEV), 0)
    own_col = jnp.sum(jnp.where(eye, own_row, 0.0), axis=1, keepdims=True)
    rank = jnp.sum(
        jnp.where(before & (own_col == own_row), 1.0, 0.0), axis=1, keepdims=True
    )
    code_col = own_col * SLOTS + rank + (col * CAP).astype(F32)
    place = iota((P_DEV, 128), 0) + 32 * (col % 4)
    code = jnp.sum(
        jnp.where(iota((P_DEV, 128), 1) == place, code_col, 0.0), axis=0, keepdims=True
    )
    code_own[...] = jnp.broadcast_to(code, (8, 128))

    pick = iota((2 * P_DEV, 2 * P_DEV), 0)
    pick = (pick % P_DEV) * 2 + pick // P_DEV == iota((2 * P_DEV, 2 * P_DEV), 1)
    parts = dot(pick.astype(F32).astype(BF16), steering[...]).astype(BF16)
    st_own[:, :BEAMS] = parts[:P_DEV]
    st_own[:, BEAMS:] = parts[P_DEV:]

    pl.semaphore_wait(barrier, COLS - 1 + ROWS - 1 + 1)

    first_sends = []
    for i in range(1, COLS):
        dest = (col + i) % COLS
        device = (g, row, dest)
        mine = pl.ds(pl.multiple_of(col * P_DEV, P_DEV), P_DEV)
        c1 = remote(code_own, code_all.at[col], code_send.at[i], code_recv.at[col], device)
        c2 = remote(st_own, st_all.at[mine], st_send.at[i], st_recv.at[col], device)
        c1.start()
        c2.start()
        first_sends += [c1, c2]
    code_all[col] = code_own[...]
    st_all[pl.ds(pl.multiple_of(col * P_DEV, P_DEV), P_DEV), :] = st_own[...]

    steps = (iota((8, 256), 0) * iota((8, 256), 1)).astype(F32) * (1.0 / NS)
    tc, ts = cos_sin(steps)
    twiddle[0] = tc
    twiddle[1] = ts
    for m in range(CHUNKS):
        lane = iota((256, 128), 1)
        d = (lane // 16) * 32 + 16 * m + lane % 16
        turns = ((iota((256, 128), 0) * d) % 256).astype(F32) * (1.0 / 256)
        c, s = cos_sin(turns)
        c, s = c.astype(BF16), s.astype(BF16)
        table[m, :256, :128] = c
        table[m, :256, 128:] = -s
        table[m, 256:, :128] = s
        table[m, 256:, 128:] = c

    scale = 1.0 / math.sqrt(NS)
    for lh in range(2):
        lanes = [pl.ds(256 * t + 128 * lh, 128) for t in range(8)]
        taper = [window[:, lanes[t]] * scale for t in range(8)]
        for pg in range(P_DEV // 16):
            rows = pl.ds(16 * pg, 16)
            xr = [raw[0, rows, lanes[t]].astype(F32) * taper[t] for t in range(8)]
            xi = [raw[1, rows, lanes[t]].astype(F32) * taper[t] for t in range(8)]
            yr, yi = dft8(xr, xi)
            for c in range(8):
                zr, zi = yr[c], yi[c]
                if c:
                    wc = twiddle[0, c : c + 1, 128 * lh : 128 * lh + 128]
                    ws = twiddle[1, c : c + 1, 128 * lh : 128 * lh + 128]
                    zr, zi = zr * wc + zi * ws, zi * wc - zr * ws
                to = pl.ds(P_DEV * c + 16 * pg, 16)
                ybuf[to, 128 * lh : 128 * lh + 128] = zr.astype(BF16)
                ybuf[to, 256 + 128 * lh : 256 + 128 * lh + 128] = zi.astype(BF16)

    z_sends = []
    for m in range(CHUNKS):
        spectrum = dot(ybuf[...], table[m])
        for part in range(2):
            tiles = swap_groups(
                [
                    spectrum[P_DEV * c : P_DEV * c + P_DEV, 128 * part : 128 * part + 128]
                    for c in range(8)
                ]
            )
            for c in range(8):
                dsend[m, c, :, 128 * part : 128 * part + 128] = tiles[c].astype(BF16)
        mine = pl.ds(pl.multiple_of(col * P_DEV, P_DEV), P_DEV)
        for i in range(1, COLS):
            dest = (col + i) % COLS
            c1 = remote(
                dsend.at[m, dest],
                zall.at[m, mine],
                z_send.at[m, i],
                z_recv.at[m, col],
                (g, row, dest),
            )
            c1.start()
            z_sends.append(c1)
        zall[m, mine, :] = dsend[m, col]

    def from_cols(wait):
        for i in range(1, COLS):
            wait((col + i) % COLS)

    def wait_first(source):
        at = pl.ds(pl.multiple_of(source * P_DEV, P_DEV), P_DEV)
        remote(
            code_own, code_all.at[source], code_send.at[0], code_recv.at[source], (g, row, source)
        ).wait_recv()
        remote(
            st_own, st_all.at[at], st_send.at[0], st_recv.at[source], (g, row, source)
        ).wait_recv()

    from_cols(wait_first)
    low = code_all[0] + code_all[1] + code_all[2] + code_all[3]
    high = code_all[4] + code_all[5] + code_all[6] + code_all[7]
    codes = jnp.concatenate([low[:1], high[:1]], axis=1).astype(I32)
    for y in range(4):
        sel[192 * y : 192 * y + 192] = jnp.where(
            iota((192, 256), 0) + 192 * y == codes, 1.0, 0.0
        ).astype(BF16)

    row_sends = []

    def to_owners(kind, data):
        mine = pl.ds(pl.multiple_of(row * SLOTS, SLOTS), SLOTS)
        for dy in (2, 1, 3, 0):
            y = (ry + dy) % 4
            block = pl.ds(pl.multiple_of(y * 4 * SLOTS, 4 * SLOTS), 4 * SLOTS)
            slots[kind, block, :] = dot(sel[block, :], data[...]).astype(BF16)
            for dx in (2, 1, 3, 0):
                dest = y * 4 + (rx + dx) % 4
                there = pl.ds(pl.multiple_of(dest * SLOTS, SLOTS), SLOTS)
                if dy == 0 and dx == 0:
                    got[kind, mine, :] = slots[kind, mine, :]
                    continue
                c1 = remote(
                    slots.at[kind, there],
                    got.at[kind, mine],
                    r_send.at[kind, 4 * dy + dx],
                    r_recv.at[kind, row],
                    (g, dest, col),
                )
                c1.start()
                row_sends.append(c1)

    def from_rows(kind):
        for i in range(1, ROWS):
            source = (row + i) % ROWS
            at = pl.ds(pl.multiple_of(source * SLOTS, SLOTS), SLOTS)
            remote(
                slots.at[kind, at],
                got.at[kind, at],
                r_send.at[kind, 0],
                r_recv.at[kind, source],
                (g, source, col),
            ).wait_recv()

    to_owners(2, st_all)

    for m in range(CHUNKS):

        def wait_z(source):
            at = pl.ds(pl.multiple_of(source * P_DEV, P_DEV), P_DEV)
            remote(
                dsend.at[m, 0],
                zall.at[m, at],
                z_send.at[m, 0],
                z_recv.at[m, source],
                (g, row, source),
            ).wait_recv()

        from_cols(wait_z)
        to_owners(m, zall.at[m])

    par[...] = jnp.zeros_like(par)
    par[0:4, :] = (interp_index[...] * HALF + beam_map[...]).astype(F32)
    par[8:12, :] = phase_offset[...]
    par[16:20, :] = phase_rate[...]
    columns = par[...].T
    bins = (col * 256 + iota((1, 256), 1)).astype(F32) * (1.0 / NS)
    for ls in range(4):
        code = columns[:, ls : ls + 1].astype(I32)
        picks[ls] = jnp.where(iota((BEAMS, Q * HALF), 1) == code, 1.0, 0.0).astype(BF16)
        angle = columns[:, 8 + ls : 9 + ls] + columns[:, 16 + ls : 17 + ls] * bins
        c, s = cos_sin(angle * (0.5 / math.pi))
        cosb[ls] = c
        sinb[ls] = s
    for q in range(Q):
        bank_nat[:, RT * q : RT * q + RT] = bank[RT * q : RT * q + RT, :]
    lane = iota((RT, RT), 0)
    order = ((lane % 16) * 8 + lane // 16 == iota((RT, RT), 1)).astype(F32).astype(BF16)
    bank_perm[...] = dot(order, bank_nat[...]).astype(BF16)

    from_rows(2)
    weights_t[...] = got[2].T

    def merge(level, m, matrices):
        lhs = jnp.concatenate(
            [child[level, m, s, :, 128 * part : 128 * part + 128] for s in range(2) for part in range(2)],
            axis=0,
        )
        v = dot(lhs, matrices[...]).astype(BF16)
        total = None
        for s in range(2):
            for part in range(2):
                at = (2 * s + part) * HALF
                for q in range(Q):
                    vbuf[s, HALF * q : HALF * q + HALF, 128 * part : 128 * part + 128] = v[
                        at : at + HALF, RT * q : RT * q + RT
                    ]
            t = dot(picks[2 * level + s], vbuf[s])
            tr, ti = t[:, :128], t[:, 128:]
            c = cosb[2 * level + s, :, 128 * m : 128 * m + 128]
            d = sinb[2 * level + s, :, 128 * m : 128 * m + 128]
            yr, yi = tr * c - ti * d, tr * d + ti * c
            total = (yr, yi) if total is None else (total[0] + yr, total[1] + yi)
        return total

    def exchange(level, m, real, imag, bit, device):
        img[level, m, :, :128] = real.astype(BF16)
        img[level, m, :, 128:] = imag.astype(BF16)
        keep = pl.ds(pl.multiple_of(bit * HALF, HALF), HALF)
        give = pl.ds(pl.multiple_of((1 - bit) * HALF, HALF), HALF)
        c1 = remote(
            img.at[level, m, give],
            child.at[level, m, bit],
            x_send.at[level, m],
            x_recv.at[level, m],
            device,
        )
        c1.start()
        child[level, m, bit] = img[level, m, keep, :]
        return c1

    def arrive(level, m, bit, device):
        remote(
            img.at[level, m, 0:HALF],
            child.at[level, m, 1 - bit],
            x_send.at[level, m],
            x_recv.at[level, m],
            device,
        ).wait_recv()

    sibling = (1 - g, row, col)
    v = row % 2
    partner = (g, row + 1 - 2 * v, col)
    x_sends = []
    for m in range(CHUNKS):
        from_rows(m)
        a = dot(weights_t[...], got[m])
        x_sends.append(
            exchange(
                0,
                m,
                a[:BEAMS, :128] - a[BEAMS:, 128:],
                a[:BEAMS, 128:] + a[BEAMS:, :128],
                g,
                sibling,
            )
        )
        arrive(0, m, g, sibling)
        real, imag = merge(0, m, bank_perm)
        x_sends.append(exchange(1, m, real, imag, v, partner))
    for m in range(CHUNKS):
        arrive(1, m, v, partner)
        real, imag = merge(1, m, bank_nat)
        outf[pl.ds(2 * m, BEAMS, stride=4), :] = real
        outf[pl.ds(2 * m + 1, BEAMS, stride=4), :] = imag
    out[...] = outf[...].astype(BF16)

    for c1 in first_sends + z_sends + row_sends + x_sends:
        c1.wait_send()


def body(
    raw_samples,
    window,
    steering,
    assignment,
    beam_map,
    interp_index,
    phase_offset,
    phase_rate,
    interp_bank,
):
    dma = pltpu.SemaphoreType.DMA
    vmem = pltpu.VMEM
    out = pl.pallas_call(
        kernel,
        out_shape=jax.ShapeDtypeStruct((4 * BEAMS, 128), BF16),
        in_specs=[pl.BlockSpec(memory_space=pltpu.VMEM)] * 9,
        out_specs=pl.BlockSpec(memory_space=pltpu.VMEM),
        scratch_shapes=[
            vmem((8 * P_DEV, 512), BF16),
            vmem((CHUNKS, 512, 256), BF16),
            vmem((2, 8, 256), F32),
            vmem((P_DEV, 256), BF16),
            vmem((COLS * P_DEV, 256), BF16),
            vmem((8, 128), F32),
            vmem((COLS, 8, 128), F32),
            vmem((CHUNKS, COLS, P_DEV, 256), BF16),
            vmem((CHUNKS, COLS * P_DEV, 256), BF16),
            vmem((ROWS * SLOTS, 256), BF16),
            vmem((3, ROWS * SLOTS, 256), BF16),
            vmem((3, ROWS * SLOTS, 256), BF16),
            vmem((256, ROWS * SLOTS), BF16),
            vmem((128, 128), F32),
            vmem((RT, Q * RT), BF16),
            vmem((RT, Q * RT), BF16),
            vmem((4, BEAMS, Q * HALF), BF16),
            vmem((4, BEAMS, 256), F32),
            vmem((4, BEAMS, 256), F32),
            vmem((2, CHUNKS, BEAMS, 256), BF16),
            vmem((2, CHUNKS, 2, HALF, 256), BF16),
            vmem((2, Q * HALF, 256), BF16),
            vmem((4 * BEAMS, 128), F32),
            dma((COLS,)),
            dma((COLS,)),
            dma((COLS,)),
            dma((COLS,)),
            dma((CHUNKS, COLS)),
            dma((CHUNKS, COLS)),
            dma((3, ROWS)),
            dma((3, ROWS)),
            dma((2, CHUNKS)),
            dma((2, CHUNKS)),
        ],
        compiler_params=pltpu.CompilerParams(
            collective_id=0, has_side_effects=True, vmem_limit_bytes=40 << 20
        ),
        name="backprojection",
    )(
        raw_samples,
        window.reshape(1, NS),
        steering.reshape(2 * P_DEV, BEAMS),
        assignment.reshape(1, P_DEV),
        beam_map.reshape(4, BEAMS),
        interp_index.reshape(4, BEAMS),
        phase_offset.reshape(4, BEAMS),
        phase_rate.reshape(4, BEAMS),
        interp_bank.reshape(Q * RT, RT),
    )
    out = out.reshape(BEAMS, CHUNKS, 2, RT).transpose(0, 2, 1, 3)
    return out.reshape(1, 1, BEAMS, 2, CHUNKS * RT)


def solution(mesh):
    in_specs = (
        P(None, ("grp", "row", "col"), None),
        P(),
        P(("grp", "row", "col"), None, None),
        P(("grp", "row", "col"), None),
        P(None, "grp", "row", None, None),
        P(None, "grp", "row", None, None),
        P(None, "grp", "row", None, None),
        P(None, "grp", "row", None, None),
        P(),
    )
    out_specs = P("grp", "row", None, None, "col")
    return jax.shard_map(body, mesh=mesh, in_specs=in_specs, out_specs=out_specs, check_vma=False)
```

```python
import math

import jax
import jax.numpy as jnp
from jax import lax
from jax.experimental import pallas as pl
from jax.experimental.pallas import tpu as pltpu
from jax.sharding import PartitionSpec as P

MESH = pl.DeviceIdType.MESH
F32, BF16, I32 = jnp.float32, jnp.bfloat16, jnp.int32

NS = 2048
BEAMS = 128
RT = 128
Q = 8
P_DEV = 32
CAP = 6
ROWS = 16
COLS = 8
SLOTS = COLS * CAP
HALF = BEAMS // 2
CHUNKS = 2

COS = (
    0.9999999890590227,
    -19.73920449945391,
    64.93911745989556,
    -85.45013953088247,
    60.16763095094928,
    -25.967599248494622,
    6.528658161366808,
)
SIN = (
    6.283185302511503,
    -41.341700405317496,
    81.60513138579344,
    -76.70301535379849,
    42.025926985567956,
    -14.89984666736486,
    3.238137509743233,
)


def horner(coefs, y):
    total = jnp.full_like(y, coefs[-1])
    for c in coefs[-2::-1]:
        total = total * y + c
    return total


def cos_sin(turns):
    r = turns - jnp.floor(turns + 0.5)
    y = r * r
    return horner(COS, y), horner(SIN, y) * r


def dft8(xr, xi):
    h = math.sqrt(0.5)
    ur = [xr[j] + xr[j + 4] for j in range(4)]
    ui = [xi[j] + xi[j + 4] for j in range(4)]
    vr = [xr[j] - xr[j + 4] for j in range(4)]
    vi = [xi[j] - xi[j + 4] for j in range(4)]
    wr = [vr[0], (vr[1] + vi[1]) * h, vi[2], (vi[3] - vr[3]) * h]
    wi = [vi[0], (vi[1] - vr[1]) * h, -vr[2], (-vr[3] - vi[3]) * h]
    yr, yi = [None] * 8, [None] * 8
    for odd, (zr, zi) in enumerate(((ur, ui), (wr, wi))):
        ar, ai = zr[0] + zr[2], zi[0] + zi[2]
        br, bi = zr[0] - zr[2], zi[0] - zi[2]
        cr, ci = zr[1] + zr[3], zi[1] + zi[3]
        dr, di = zr[1] - zr[3], zi[1] - zi[3]
        yr[odd], yi[odd] = ar + cr, ai + ci
        yr[odd + 4], yi[odd + 4] = ar - cr, ai - ci
        yr[odd + 2], yi[odd + 2] = br + di, bi - dr
        yr[odd + 6], yi[odd + 6] = br - di, bi + dr
    return yr, yi


def swap_groups(tiles):
    group = lax.broadcasted_iota(I32, tiles[0].shape, 1) // 16
    tiles = list(tiles)
    for bit in range(3):
        step = 1 << bit
        upper = (group // step) % 2 == 1
        for a in range(8):
            if a & step:
                continue
            low, high = tiles[a], tiles[a + step]
            tiles[a] = jnp.where(upper, pltpu.roll(high, 16 * step, 1), low)
            tiles[a + step] = jnp.where(upper, high, pltpu.roll(low, 128 - 16 * step, 1))
    return tiles


def dot(a, b):
    return jnp.dot(a, b, preferred_element_type=F32)


def iota(shape, dim):
    return lax.broadcasted_iota(I32, shape, dim)


def kernel(
    raw_in,
    window_in,
    steering_in,
    assignment_in,
    beam_map_in,
    interp_index_in,
    phase_offset_in,
    phase_rate_in,
    bank_in,
    out,
    raw,
    window,
    steering,
    assignment,
    beam_map,
    interp_index,
    phase_offset,
    phase_rate,
    bank,
    ybuf,
    table,
    twiddle,
    st_own,
    st_all,
    code_own,
    code_all,
    dsend,
    zall,
    sel,
    slots,
    got,
    w_slots,
    w_got,
    weights_t,
    par,
    bank_nat,
    bank_perm,
    picks,
    cosb,
    sinb,
    img,
    child,
    vbuf,
    outf,
    in_sems,
    st_send,
    st_recv,
    code_send,
    code_recv,
    z_send,
    z_recv,
    r_send,
    r_recv,
    p_send,
    p_recv,
    x_send,
    x_recv,
):
    g, row, col = lax.axis_index("grp"), lax.axis_index("row"), lax.axis_index("col")
    ry, rx = row // 4, row % 4

    def remote(src, dst, ssem, rsem, device):
        return pltpu.make_async_remote_copy(
            src_ref=src,
            dst_ref=dst,
            send_sem=ssem,
            recv_sem=rsem,
            device_id=device,
            device_id_type=MESH,
        )

    loads = [
        pltpu.make_async_copy(src, dst, in_sems.at[i])
        for i, (src, dst) in enumerate(
            (
                (assignment_in, assignment),
                (steering_in, steering),
                (window_in, window),
                (raw_in, raw),
                (beam_map_in, beam_map),
                (interp_index_in, interp_index),
                (phase_offset_in, phase_offset),
                (phase_rate_in, phase_rate),
                (bank_in, bank),
            )
        )
    ]
    for load in loads:
        load.start()

    barrier = pltpu.get_barrier_semaphore()

    def greet_col(i, _):
        pl.semaphore_signal(
            barrier, inc=1, device_id=(g, row, (col + i) % COLS), device_id_type=MESH
        )
        return 0

    def greet_row(i, _):
        pl.semaphore_signal(
            barrier, inc=1, device_id=(g, (row + i) % ROWS, col), device_id_type=MESH
        )
        return 0

    lax.fori_loop(1, COLS, greet_col, 0)
    lax.fori_loop(1, ROWS, greet_row, 0)
    pl.semaphore_signal(barrier, inc=1, device_id=(1 - g, row, col), device_id_type=MESH)

    loads[0].wait()
    own_row = assignment[...].astype(F32)
    eye = iota((P_DEV, P_DEV), 0) == iota((P_DEV, P_DEV), 1)
    before = iota((P_DEV, P_DEV), 1) < iota((P_DEV, P_DEV), 0)
    own_col = jnp.sum(jnp.where(eye, own_row, 0.0), axis=1, keepdims=True)
    rank = jnp.sum(
        jnp.where(before & (own_col == own_row), 1.0, 0.0), axis=1, keepdims=True
    )
    code_col = own_col * SLOTS + rank + (col * CAP).astype(F32)
    place = iota((P_DEV, 128), 0) + 32 * (col % 4)
    code = jnp.sum(
        jnp.where(iota((P_DEV, 128), 1) == place, code_col, 0.0), axis=0, keepdims=True
    )
    code_own[...] = code

    loads[1].wait()
    pick = iota((2 * P_DEV, 2 * P_DEV), 0)
    pick = (pick % P_DEV) * 2 + pick // P_DEV == iota((2 * P_DEV, 2 * P_DEV), 1)
    parts = dot(pick.astype(F32).astype(BF16), steering[...]).astype(BF16)
    st_own[0] = parts[:P_DEV]
    st_own[1] = parts[P_DEV:]

    pl.semaphore_wait(barrier, COLS - 1 + ROWS - 1 + 1)

    parity = col % 2
    first_sends = []
    for i in range(1, COLS):
        dest = (col + i) % COLS
        device = (g, row, dest)
        mine = pl.ds(pl.multiple_of(col * P_DEV, P_DEV), P_DEV)
        c1 = remote(code_own, code_all.at[col], code_send.at[i], code_recv.at[col], device)
        c2 = remote(st_own.at[dest % 2], st_all.at[mine], st_send.at[i], st_recv.at[col], device)
        c1.start()
        c2.start()
        first_sends += [c1, c2]
    code_all[col] = code_own[...]
    st_all[pl.ds(pl.multiple_of(col * P_DEV, P_DEV), P_DEV), :] = st_own[parity]

    steps = (iota((8, 256), 0) * iota((8, 256), 1)).astype(F32) * (1.0 / NS)
    tc, ts = cos_sin(steps)
    twiddle[0] = tc
    twiddle[1] = ts
    for m in range(CHUNKS):
        lane = iota((256, 128), 1)
        d = (lane // 16) * 32 + 16 * m + lane % 16
        turns = ((iota((256, 128), 0) * d) % 256).astype(F32) * (1.0 / 256)
        c, s = cos_sin(turns)
        c, s = c.astype(BF16), s.astype(BF16)
        table[m, :256, :128] = c
        table[m, :256, 128:] = -s
        table[m, 256:, :128] = s
        table[m, 256:, 128:] = c

    loads[2].wait()
    loads[3].wait()
    scale = 1.0 / math.sqrt(NS)
    for lh in range(2):
        lanes = [pl.ds(256 * t + 128 * lh, 128) for t in range(8)]
        taper = [window[:, lanes[t]] * scale for t in range(8)]
        for pg in range(P_DEV // 16):
            rows = pl.ds(16 * pg, 16)
            xr = [raw[0, rows, lanes[t]].astype(F32) * taper[t] for t in range(8)]
            xi = [raw[1, rows, lanes[t]].astype(F32) * taper[t] for t in range(8)]
            yr, yi = dft8(xr, xi)
            for c in range(8):
                zr, zi = yr[c], yi[c]
                if c:
                    wc = twiddle[0, c : c + 1, 128 * lh : 128 * lh + 128]
                    ws = twiddle[1, c : c + 1, 128 * lh : 128 * lh + 128]
                    zr, zi = zr * wc + zi * ws, zi * wc - zr * ws
                to = pl.ds(P_DEV * c + 16 * pg, 16)
                ybuf[to, 128 * lh : 128 * lh + 128] = zr.astype(BF16)
                ybuf[to, 256 + 128 * lh : 256 + 128 * lh + 128] = zi.astype(BF16)

    z_sends = []
    for m in range(CHUNKS):
        spectrum = dot(ybuf[...], table[m])
        for part in range(2):
            tiles = swap_groups(
                [
                    spectrum[P_DEV * c : P_DEV * c + P_DEV, 128 * part : 128 * part + 128]
                    for c in range(8)
                ]
            )
            for c in range(8):
                dsend[m, c, :, 128 * part : 128 * part + 128] = tiles[c].astype(BF16)
        mine = pl.ds(pl.multiple_of(col * P_DEV, P_DEV), P_DEV)
        for i in range(1, COLS):
            dest = (col + i) % COLS
            c1 = remote(
                dsend.at[m, dest],
                zall.at[m, mine],
                z_send.at[m, i],
                z_recv.at[m, col],
                (g, row, dest),
            )
            c1.start()
            z_sends.append(c1)
        zall[m, mine, :] = dsend[m, col]

    def from_cols(wait):
        for i in range(1, COLS):
            wait((col + i) % COLS)

    def wait_first(source):
        at = pl.ds(pl.multiple_of(source * P_DEV, P_DEV), P_DEV)
        remote(
            code_own, code_all.at[source], code_send.at[0], code_recv.at[source], (g, row, source)
        ).wait_recv()
        remote(
            st_own.at[0], st_all.at[at], st_send.at[0], st_recv.at[source], (g, row, source)
        ).wait_recv()

    from_cols(wait_first)
    low = code_all[0] + code_all[1] + code_all[2] + code_all[3]
    high = code_all[4] + code_all[5] + code_all[6] + code_all[7]
    codes = jnp.concatenate([low, high], axis=1).astype(I32)
    for y in range(4):
        sel[192 * y : 192 * y + 192] = jnp.where(
            iota((192, 256), 0) + 192 * y == codes, 1.0, 0.0
        ).astype(BF16)

    row_sends = []

    def to_owners(kind, data, packed, landed):
        mine = pl.ds(pl.multiple_of(row * SLOTS, SLOTS), SLOTS)
        for dy in (2, 1, 3, 0):
            y = (ry + dy) % 4
            block = pl.ds(pl.multiple_of(y * 4 * SLOTS, 4 * SLOTS), 4 * SLOTS)
            packed[block, :] = dot(sel[block, :], data[...]).astype(BF16)
            for dx in (2, 1, 3, 0):
                dest = y * 4 + (rx + dx) % 4
                there = pl.ds(pl.multiple_of(dest * SLOTS, SLOTS), SLOTS)
                if dy == 0 and dx == 0:
                    landed[mine, :] = packed[mine, :]
                    continue
                c1 = remote(
                    packed.at[there],
                    landed.at[mine],
                    r_send.at[kind, 4 * dy + dx],
                    r_recv.at[kind, row],
                    (g, dest, col),
                )
                c1.start()
                row_sends.append(c1)

    def from_rows(kind, packed, landed, dys=(2, 1, 3, 0)):
        for dy in dys:
            for dx in (2, 1, 3, 0):
                if dy == 0 and dx == 0:
                    continue
                source = (ry - dy + 4) % 4 * 4 + (rx - dx + 4) % 4
                at = pl.ds(pl.multiple_of(source * SLOTS, SLOTS), SLOTS)
                remote(
                    packed.at[at],
                    landed.at[at],
                    r_send.at[kind, 0],
                    r_recv.at[kind, source],
                    (g, source, col),
                ).wait_recv()

    def col_pass(i, part):
        y = (ry - i + 4) % 4
        block = pl.ds(pl.multiple_of(y * 4 * SLOTS, 4 * SLOTS), 4 * SLOTS)
        return remote(
            w_got.at[part, block],
            w_got.at[part, block],
            p_send.at[i],
            p_recv.at[i],
            (g, row, col + 1 - 2 * parity),
        )

    to_owners(2, st_all, w_slots, w_got.at[parity])

    for m in range(CHUNKS):

        def wait_z(source):
            at = pl.ds(pl.multiple_of(source * P_DEV, P_DEV), P_DEV)
            remote(
                dsend.at[m, 0],
                zall.at[m, at],
                z_send.at[m, 0],
                z_recv.at[m, source],
                (g, row, source),
            ).wait_recv()

        from_cols(wait_z)
        to_owners(m, zall.at[m], slots.at[m], got.at[m])
        if m == 0:
            for dy in (2, 1, 3, 0):
                from_rows(2, w_slots, w_got.at[parity], (dy,))
                c1 = col_pass(dy, parity)
                c1.start()
                row_sends.append(c1)

    for load in loads[4:]:
        load.wait()
    par[...] = jnp.zeros_like(par)
    par[0:4, :] = (interp_index[...] * HALF + beam_map[...]).astype(F32)
    par[8:12, :] = phase_offset[...]
    par[16:20, :] = phase_rate[...]
    columns = par[...].T
    bins = (col * 256 + iota((1, 256), 1)).astype(F32) * (1.0 / NS)
    for ls in range(4):
        code = columns[:, ls : ls + 1].astype(I32)
        picks[ls] = jnp.where(iota((BEAMS, Q * HALF), 1) == code, 1.0, 0.0).astype(BF16)
        angle = columns[:, 8 + ls : 9 + ls] + columns[:, 16 + ls : 17 + ls] * bins
        c, s = cos_sin(angle * (0.5 / math.pi))
        cosb[ls] = c
        sinb[ls] = s
    for q in range(Q):
        bank_nat[:, RT * q : RT * q + RT] = bank[RT * q : RT * q + RT, :]
    lane = iota((RT, RT), 0)
    order = ((lane % 16) * 8 + lane // 16 == iota((RT, RT), 1)).astype(F32).astype(BF16)
    bank_perm[...] = dot(order, bank_nat[...]).astype(BF16)

    for dy in (2, 1, 3, 0):
        col_pass(dy, 1 - parity).wait_recv()
    weights_t[:BEAMS] = w_got[0].T
    weights_t[BEAMS:] = w_got[1].T

    def merge(level, m, matrices):
        lhs = jnp.concatenate(
            [child[level, m, s, :, 128 * part : 128 * part + 128] for s in range(2) for part in range(2)],
            axis=0,
        )
        v = dot(lhs, matrices[...]).astype(BF16)
        total = None
        for s in range(2):
            for part in range(2):
                at = (2 * s + part) * HALF
                for q in range(Q):
                    vbuf[s, HALF * q : HALF * q + HALF, 128 * part : 128 * part + 128] = v[
                        at : at + HALF, RT * q : RT * q + RT
                    ]
            t = dot(picks[2 * level + s], vbuf[s])
            tr, ti = t[:, :128], t[:, 128:]
            c = cosb[2 * level + s, :, 128 * m : 128 * m + 128]
            d = sinb[2 * level + s, :, 128 * m : 128 * m + 128]
            yr, yi = tr * c - ti * d, tr * d + ti * c
            total = (yr, yi) if total is None else (total[0] + yr, total[1] + yi)
        return total

    def exchange(level, m, real, imag, bit, device):
        img[level, m, :, :128] = real.astype(BF16)
        img[level, m, :, 128:] = imag.astype(BF16)
        keep = pl.ds(pl.multiple_of(bit * HALF, HALF), HALF)
        give = pl.ds(pl.multiple_of((1 - bit) * HALF, HALF), HALF)
        c1 = remote(
            img.at[level, m, give],
            child.at[level, m, bit],
            x_send.at[level, m],
            x_recv.at[level, m],
            device,
        )
        c1.start()
        child[level, m, bit] = img[level, m, keep, :]
        return c1

    def arrive(level, m, bit, device):
        remote(
            img.at[level, m, 0:HALF],
            child.at[level, m, 1 - bit],
            x_send.at[level, m],
            x_recv.at[level, m],
            device,
        ).wait_recv()

    sibling = (1 - g, row, col)
    v = row % 2
    partner = (g, row + 1 - 2 * v, col)
    x_sends = []
    for m in range(CHUNKS):
        from_rows(m, slots.at[m], got.at[m])
        a = dot(weights_t[...], got[m])
        x_sends.append(
            exchange(
                0,
                m,
                a[:BEAMS, :128] - a[BEAMS:, 128:],
                a[:BEAMS, 128:] + a[BEAMS:, :128],
                g,
                sibling,
            )
        )
        arrive(0, m, g, sibling)
        real, imag = merge(0, m, bank_perm)
        x_sends.append(exchange(1, m, real, imag, v, partner))
    for m in range(CHUNKS):
        arrive(1, m, v, partner)
        real, imag = merge(1, m, bank_nat)
        outf[pl.ds(2 * m, BEAMS, stride=4), :] = real
        outf[pl.ds(2 * m + 1, BEAMS, stride=4), :] = imag
    out[...] = outf[...].astype(BF16)

    for c1 in first_sends + z_sends + row_sends + x_sends:
        c1.wait_send()


def body(
    raw_samples,
    window,
    steering,
    assignment,
    beam_map,
    interp_index,
    phase_offset,
    phase_rate,
    interp_bank,
):
    dma = pltpu.SemaphoreType.DMA
    vmem = pltpu.VMEM
    out = pl.pallas_call(
        kernel,
        out_shape=jax.ShapeDtypeStruct((4 * BEAMS, 128), BF16),
        in_specs=[pl.BlockSpec(memory_space=pltpu.HBM)] * 9,
        out_specs=pl.BlockSpec(memory_space=pltpu.VMEM),
        scratch_shapes=[
            vmem((2, P_DEV, NS), BF16),
            vmem((1, NS), F32),
            vmem((2 * P_DEV, BEAMS), BF16),
            vmem((1, P_DEV), I32),
            vmem((4, BEAMS), I32),
            vmem((4, BEAMS), I32),
            vmem((4, BEAMS), F32),
            vmem((4, BEAMS), F32),
            vmem((Q * RT, RT), BF16),
            vmem((8 * P_DEV, 512), BF16),
            vmem((CHUNKS, 512, 256), BF16),
            vmem((2, 8, 256), F32),
            vmem((2, P_DEV, BEAMS), BF16),
            vmem((COLS * P_DEV, BEAMS), BF16),
            vmem((1, 128), F32),
            vmem((COLS, 1, 128), F32),
            vmem((CHUNKS, COLS, P_DEV, 256), BF16),
            vmem((CHUNKS, COLS * P_DEV, 256), BF16),
            vmem((ROWS * SLOTS, 256), BF16),
            vmem((CHUNKS, ROWS * SLOTS, 256), BF16),
            vmem((CHUNKS, ROWS * SLOTS, 256), BF16),
            vmem((ROWS * SLOTS, BEAMS), BF16),
            vmem((2, ROWS * SLOTS, BEAMS), BF16),
            vmem((256, ROWS * SLOTS), BF16),
            vmem((128, 128), F32),
            vmem((RT, Q * RT), BF16),
            vmem((RT, Q * RT), BF16),
            vmem((4, BEAMS, Q * HALF), BF16),
            vmem((4, BEAMS, 256), F32),
            vmem((4, BEAMS, 256), F32),
            vmem((2, CHUNKS, BEAMS, 256), BF16),
            vmem((2, CHUNKS, 2, HALF, 256), BF16),
            vmem((2, Q * HALF, 256), BF16),
            vmem((4 * BEAMS, 128), F32),
            dma((9,)),
            dma((COLS,)),
            dma((COLS,)),
            dma((COLS,)),
            dma((COLS,)),
            dma((CHUNKS, COLS)),
            dma((CHUNKS, COLS)),
            dma((3, ROWS)),
            dma((3, ROWS)),
            dma((4,)),
            dma((4,)),
            dma((2, CHUNKS)),
            dma((2, CHUNKS)),
        ],
        compiler_params=pltpu.CompilerParams(
            collective_id=0, has_side_effects=True, vmem_limit_bytes=56 << 20
        ),
        name="backprojection",
    )(
        raw_samples,
        window.reshape(1, NS),
        steering.reshape(2 * P_DEV, BEAMS),
        assignment.reshape(1, P_DEV),
        beam_map.reshape(4, BEAMS),
        interp_index.reshape(4, BEAMS),
        phase_offset.reshape(4, BEAMS),
        phase_rate.reshape(4, BEAMS),
        interp_bank.reshape(Q * RT, RT),
    )
    out = out.reshape(BEAMS, CHUNKS, 2, RT).transpose(0, 2, 1, 3)
    return out.reshape(1, 1, BEAMS, 2, CHUNKS * RT)


def solution(mesh):
    in_specs = (
        P(None, ("grp", "row", "col"), None),
        P(),
        P(("grp", "row", "col"), None, None),
        P(("grp", "row", "col"), None),
        P(None, "grp", "row", None, None),
        P(None, "grp", "row", None, None),
        P(None, "grp", "row", None, None),
        P(None, "grp", "row", None, None),
        P(),
    )
    out_specs = P("grp", "row", None, None, "col")
    return jax.shard_map(body, mesh=mesh, in_specs=in_specs, out_specs=out_specs, check_vma=False)
```

```python
import math

import jax
import jax.numpy as jnp
from jax import lax
from jax.experimental import pallas as pl
from jax.experimental.pallas import tpu as pltpu
from jax.sharding import PartitionSpec as P

MESH = pl.DeviceIdType.MESH
F32, BF16, I32 = jnp.float32, jnp.bfloat16, jnp.int32

NS = 2048
BEAMS = 128
RT = 128
Q = 8
P_DEV = 32
CAP = 6
ROWS = 16
COLS = 8
SLOTS = COLS * CAP
HALF = BEAMS // 2
CHUNKS = 2

COS = (
    0.9999999890590227,
    -19.73920449945391,
    64.93911745989556,
    -85.45013953088247,
    60.16763095094928,
    -25.967599248494622,
    6.528658161366808,
)
SIN = (
    6.283185302511503,
    -41.341700405317496,
    81.60513138579344,
    -76.70301535379849,
    42.025926985567956,
    -14.89984666736486,
    3.238137509743233,
)


def horner(coefs, y):
    total = jnp.full_like(y, coefs[-1])
    for c in coefs[-2::-1]:
        total = total * y + c
    return total


def cos_sin(turns):
    r = turns - jnp.floor(turns + 0.5)
    y = r * r
    return horner(COS, y), horner(SIN, y) * r


def dft8(xr, xi):
    h = math.sqrt(0.5)
    ur = [xr[j] + xr[j + 4] for j in range(4)]
    ui = [xi[j] + xi[j + 4] for j in range(4)]
    vr = [xr[j] - xr[j + 4] for j in range(4)]
    vi = [xi[j] - xi[j + 4] for j in range(4)]
    wr = [vr[0], (vr[1] + vi[1]) * h, vi[2], (vi[3] - vr[3]) * h]
    wi = [vi[0], (vi[1] - vr[1]) * h, -vr[2], (-vr[3] - vi[3]) * h]
    yr, yi = [None] * 8, [None] * 8
    for odd, (zr, zi) in enumerate(((ur, ui), (wr, wi))):
        ar, ai = zr[0] + zr[2], zi[0] + zi[2]
        br, bi = zr[0] - zr[2], zi[0] - zi[2]
        cr, ci = zr[1] + zr[3], zi[1] + zi[3]
        dr, di = zr[1] - zr[3], zi[1] - zi[3]
        yr[odd], yi[odd] = ar + cr, ai + ci
        yr[odd + 4], yi[odd + 4] = ar - cr, ai - ci
        yr[odd + 2], yi[odd + 2] = br + di, bi - dr
        yr[odd + 6], yi[odd + 6] = br - di, bi + dr
    return yr, yi


def swap_groups(tiles):
    group = lax.broadcasted_iota(I32, tiles[0].shape, 1) // 16
    tiles = list(tiles)
    for bit in range(3):
        step = 1 << bit
        upper = (group // step) % 2 == 1
        for a in range(8):
            if a & step:
                continue
            low, high = tiles[a], tiles[a + step]
            tiles[a] = jnp.where(upper, pltpu.roll(high, 16 * step, 1), low)
            tiles[a + step] = jnp.where(upper, high, pltpu.roll(low, 128 - 16 * step, 1))
    return tiles


def dot(a, b):
    return jnp.dot(a, b, preferred_element_type=F32)


def iota(shape, dim):
    return lax.broadcasted_iota(I32, shape, dim)


def kernel(
    raw_in,
    window_in,
    steering_in,
    assignment_in,
    beam_map_in,
    interp_index_in,
    phase_offset_in,
    phase_rate_in,
    bank_in,
    out,
    raw,
    window,
    steering,
    assignment,
    beam_map,
    interp_index,
    phase_offset,
    phase_rate,
    bank,
    ybuf,
    table,
    twiddle,
    st_own,
    st_all,
    code_own,
    code_all,
    dsend,
    zall,
    sel,
    slots,
    got,
    w_slots,
    w_got,
    weights_t,
    par,
    bank_nat,
    bank_perm,
    picks,
    cosb,
    sinb,
    img,
    child,
    vbuf,
    outf,
    in_sems,
    st_send,
    st_recv,
    code_send,
    code_recv,
    z_send,
    z_recv,
    r_send,
    r_recv,
    p_send,
    p_recv,
    x_send,
    x_recv,
):
    g, row, col = lax.axis_index("grp"), lax.axis_index("row"), lax.axis_index("col")
    ry, rx = row // 4, row % 4

    def remote(src, dst, ssem, rsem, device):
        return pltpu.make_async_remote_copy(
            src_ref=src,
            dst_ref=dst,
            send_sem=ssem,
            recv_sem=rsem,
            device_id=device,
            device_id_type=MESH,
        )

    loads = [
        pltpu.make_async_copy(src, dst, in_sems.at[i])
        for i, (src, dst) in enumerate(
            (
                (assignment_in, assignment),
                (steering_in, steering),
                (window_in, window),
                (raw_in, raw),
                (beam_map_in, beam_map),
                (interp_index_in, interp_index),
                (phase_offset_in, phase_offset),
                (phase_rate_in, phase_rate),
                (bank_in, bank),
            )
        )
    ]
    for load in loads:
        load.start()

    barrier = pltpu.get_barrier_semaphore()

    def greet_col(i, _):
        pl.semaphore_signal(
            barrier, inc=1, device_id=(g, row, (col + i) % COLS), device_id_type=MESH
        )
        return 0

    def greet_row(i, _):
        pl.semaphore_signal(
            barrier, inc=1, device_id=(g, (row + i) % ROWS, col), device_id_type=MESH
        )
        return 0

    lax.fori_loop(1, COLS, greet_col, 0)
    lax.fori_loop(1, ROWS, greet_row, 0)
    pl.semaphore_signal(barrier, inc=1, device_id=(1 - g, row, col), device_id_type=MESH)

    steps = (iota((8, 256), 0) * iota((8, 256), 1)).astype(F32) * (1.0 / NS)
    tc, ts = cos_sin(steps)
    twiddle[0] = tc
    twiddle[1] = ts
    for m in range(CHUNKS):
        lane = iota((256, 128), 1)
        d = (lane // 16) * 32 + 16 * m + lane % 16
        turns = ((iota((256, 128), 0) * d) % 256).astype(F32) * (1.0 / 256)
        c, s = cos_sin(turns)
        c, s = c.astype(BF16), s.astype(BF16)
        table[m, :256, :128] = c
        table[m, :256, 128:] = -s
        table[m, 256:, :128] = s
        table[m, 256:, 128:] = c

    loads[0].wait()
    own_row = assignment[...].astype(F32)
    eye = iota((P_DEV, P_DEV), 0) == iota((P_DEV, P_DEV), 1)
    before = iota((P_DEV, P_DEV), 1) < iota((P_DEV, P_DEV), 0)
    own_col = jnp.sum(jnp.where(eye, own_row, 0.0), axis=1, keepdims=True)
    rank = jnp.sum(
        jnp.where(before & (own_col == own_row), 1.0, 0.0), axis=1, keepdims=True
    )
    code_col = own_col * SLOTS + rank + (col * CAP).astype(F32)
    place = iota((P_DEV, 128), 0) + 32 * (col % 4)
    code = jnp.sum(
        jnp.where(iota((P_DEV, 128), 1) == place, code_col, 0.0), axis=0, keepdims=True
    )
    code_own[...] = code

    loads[1].wait()
    pick = iota((2 * P_DEV, 2 * P_DEV), 0)
    pick = (pick % P_DEV) * 2 + pick // P_DEV == iota((2 * P_DEV, 2 * P_DEV), 1)
    parts = dot(pick.astype(F32).astype(BF16), steering[...]).astype(BF16)
    st_own[0] = parts[:P_DEV]
    st_own[1] = parts[P_DEV:]

    pl.semaphore_wait(barrier, COLS - 1 + ROWS - 1 + 1)

    parity = col % 2
    first_sends = []
    for i in range(1, COLS):
        dest = (col + i) % COLS
        device = (g, row, dest)
        mine = pl.ds(pl.multiple_of(col * P_DEV, P_DEV), P_DEV)
        c1 = remote(code_own, code_all.at[col], code_send.at[i], code_recv.at[col], device)
        c2 = remote(st_own.at[dest % 2], st_all.at[mine], st_send.at[i], st_recv.at[col], device)
        c1.start()
        c2.start()
        first_sends += [c1, c2]
    code_all[col] = code_own[...]
    st_all[pl.ds(pl.multiple_of(col * P_DEV, P_DEV), P_DEV), :] = st_own[parity]

    loads[2].wait()
    loads[3].wait()
    scale = 1.0 / math.sqrt(NS)
    for lh in range(2):
        lanes = [pl.ds(256 * t + 128 * lh, 128) for t in range(8)]
        taper = [window[:, lanes[t]] * scale for t in range(8)]
        for pg in range(P_DEV // 16):
            rows = pl.ds(16 * pg, 16)
            xr = [raw[0, rows, lanes[t]].astype(F32) * taper[t] for t in range(8)]
            xi = [raw[1, rows, lanes[t]].astype(F32) * taper[t] for t in range(8)]
            yr, yi = dft8(xr, xi)
            for c in range(8):
                zr, zi = yr[c], yi[c]
                if c:
                    wc = twiddle[0, c : c + 1, 128 * lh : 128 * lh + 128]
                    ws = twiddle[1, c : c + 1, 128 * lh : 128 * lh + 128]
                    zr, zi = zr * wc + zi * ws, zi * wc - zr * ws
                to = pl.ds(P_DEV * c + 16 * pg, 16)
                ybuf[to, 128 * lh : 128 * lh + 128] = zr.astype(BF16)
                ybuf[to, 256 + 128 * lh : 256 + 128 * lh + 128] = zi.astype(BF16)

    z_sends = []
    for m in range(CHUNKS):
        spectrum = dot(ybuf[...], table[m])
        for part in range(2):
            tiles = swap_groups(
                [
                    spectrum[P_DEV * c : P_DEV * c + P_DEV, 128 * part : 128 * part + 128]
                    for c in range(8)
                ]
            )
            for c in range(8):
                dsend[m, c, :, 128 * part : 128 * part + 128] = tiles[c].astype(BF16)

    def to_cols(m):
        mine = pl.ds(pl.multiple_of(col * P_DEV, P_DEV), P_DEV)
        for i in (4, 3, 5, 2, 6, 1, 7):
            dest = (col + i) % COLS
            c1 = remote(
                dsend.at[m, dest],
                zall.at[m, mine],
                z_send.at[m, i],
                z_recv.at[m, col],
                (g, row, dest),
            )
            c1.start()
            z_sends.append(c1)
        zall[m, mine, :] = dsend[m, col]

    to_cols(0)

    def from_cols(wait):
        for i in range(1, COLS):
            wait((col + i) % COLS)

    def wait_first(source):
        at = pl.ds(pl.multiple_of(source * P_DEV, P_DEV), P_DEV)
        remote(
            code_own, code_all.at[source], code_send.at[0], code_recv.at[source], (g, row, source)
        ).wait_recv()
        remote(
            st_own.at[0], st_all.at[at], st_send.at[0], st_recv.at[source], (g, row, source)
        ).wait_recv()

    from_cols(wait_first)
    low = code_all[0] + code_all[1] + code_all[2] + code_all[3]
    high = code_all[4] + code_all[5] + code_all[6] + code_all[7]
    codes = jnp.concatenate([low, high], axis=1).astype(I32)
    for y in range(4):
        sel[192 * y : 192 * y + 192] = jnp.where(
            iota((192, 256), 0) + 192 * y == codes, 1.0, 0.0
        ).astype(BF16)

    row_sends = []

    def to_owners(kind, data, packed, landed):
        mine = pl.ds(pl.multiple_of(row * SLOTS, SLOTS), SLOTS)
        for dy in (2, 1, 3, 0):
            y = (ry + dy) % 4
            block = pl.ds(pl.multiple_of(y * 4 * SLOTS, 4 * SLOTS), 4 * SLOTS)
            packed[block, :] = dot(sel[block, :], data[...]).astype(BF16)
            for dx in (2, 1, 3, 0):
                dest = y * 4 + (rx + dx) % 4
                there = pl.ds(pl.multiple_of(dest * SLOTS, SLOTS), SLOTS)
                if dy == 0 and dx == 0:
                    landed[mine, :] = packed[mine, :]
                    continue
                c1 = remote(
                    packed.at[there],
                    landed.at[mine],
                    r_send.at[kind, 4 * dy + dx],
                    r_recv.at[kind, row],
                    (g, dest, col),
                )
                c1.start()
                row_sends.append(c1)

    def from_rows(kind, packed, landed, dys=(2, 1, 3, 0)):
        for dy in dys:
            for dx in (2, 1, 3, 0):
                if dy == 0 and dx == 0:
                    continue
                source = (ry - dy + 4) % 4 * 4 + (rx - dx + 4) % 4
                at = pl.ds(pl.multiple_of(source * SLOTS, SLOTS), SLOTS)
                remote(
                    packed.at[at],
                    landed.at[at],
                    r_send.at[kind, 0],
                    r_recv.at[kind, source],
                    (g, source, col),
                ).wait_recv()

    def col_pass(i, part):
        y = (ry - i + 4) % 4
        block = pl.ds(pl.multiple_of(y * 4 * SLOTS, 4 * SLOTS), 4 * SLOTS)
        return remote(
            w_got.at[part, block],
            w_got.at[part, block],
            p_send.at[i],
            p_recv.at[i],
            (g, row, col + 1 - 2 * parity),
        )

    to_owners(2, st_all, w_slots, w_got.at[parity])
    to_cols(1)

    for m in range(CHUNKS):

        def wait_z(source):
            at = pl.ds(pl.multiple_of(source * P_DEV, P_DEV), P_DEV)
            remote(
                dsend.at[m, 0],
                zall.at[m, at],
                z_send.at[m, 0],
                z_recv.at[m, source],
                (g, row, source),
            ).wait_recv()

        from_cols(wait_z)
        to_owners(m, zall.at[m], slots.at[m], got.at[m])
        if m == 0:
            for dy in (2, 1, 3, 0):
                from_rows(2, w_slots, w_got.at[parity], (dy,))
                c1 = col_pass(dy, parity)
                c1.start()
                row_sends.append(c1)

    for load in loads[4:]:
        load.wait()
    par[...] = jnp.zeros_like(par)
    par[0:4, :] = (interp_index[...] * HALF + beam_map[...]).astype(F32)
    par[8:12, :] = phase_offset[...]
    par[16:20, :] = phase_rate[...]
    columns = par[...].T
    bins = (col * 256 + iota((1, 256), 1)).astype(F32) * (1.0 / NS)
    for ls in range(4):
        code = columns[:, ls : ls + 1].astype(I32)
        picks[ls] = jnp.where(iota((BEAMS, Q * HALF), 1) == code, 1.0, 0.0).astype(BF16)
        angle = columns[:, 8 + ls : 9 + ls] + columns[:, 16 + ls : 17 + ls] * bins
        c, s = cos_sin(angle * (0.5 / math.pi))
        cosb[ls] = c
        sinb[ls] = s
    for q in range(Q):
        bank_nat[:, RT * q : RT * q + RT] = bank[RT * q : RT * q + RT, :]
    lane = iota((RT, RT), 0)
    order = ((lane % 16) * 8 + lane // 16 == iota((RT, RT), 1)).astype(F32).astype(BF16)
    bank_perm[...] = dot(order, bank_nat[...]).astype(BF16)

    for dy in (2, 1, 3, 0):
        col_pass(dy, 1 - parity).wait_recv()
    weights_t[:BEAMS] = w_got[0].T
    weights_t[BEAMS:] = w_got[1].T

    def merge(level, m, matrices):
        lhs = jnp.concatenate(
            [child[level, m, s, :, 128 * part : 128 * part + 128] for s in range(2) for part in range(2)],
            axis=0,
        )
        v = dot(lhs, matrices[...]).astype(BF16)
        total = None
        for s in range(2):
            for part in range(2):
                at = (2 * s + part) * HALF
                for q in range(Q):
                    vbuf[s, HALF * q : HALF * q + HALF, 128 * part : 128 * part + 128] = v[
                        at : at + HALF, RT * q : RT * q + RT
                    ]
            t = dot(picks[2 * level + s], vbuf[s])
            tr, ti = t[:, :128], t[:, 128:]
            c = cosb[2 * level + s, :, 128 * m : 128 * m + 128]
            d = sinb[2 * level + s, :, 128 * m : 128 * m + 128]
            yr, yi = tr * c - ti * d, tr * d + ti * c
            total = (yr, yi) if total is None else (total[0] + yr, total[1] + yi)
        return total

    def exchange(level, m, real, imag, bit, device):
        img[level, m, :, :128] = real.astype(BF16)
        img[level, m, :, 128:] = imag.astype(BF16)
        keep = pl.ds(pl.multiple_of(bit * HALF, HALF), HALF)
        give = pl.ds(pl.multiple_of((1 - bit) * HALF, HALF), HALF)
        c1 = remote(
            img.at[level, m, give],
            child.at[level, m, bit],
            x_send.at[level, m],
            x_recv.at[level, m],
            device,
        )
        c1.start()
        child[level, m, bit] = img[level, m, keep, :]
        return c1

    def arrive(level, m, bit, device):
        remote(
            img.at[level, m, 0:HALF],
            child.at[level, m, 1 - bit],
            x_send.at[level, m],
            x_recv.at[level, m],
            device,
        ).wait_recv()

    sibling = (1 - g, row, col)
    v = row % 2
    partner = (g, row + 1 - 2 * v, col)
    x_sends = []
    for m in range(CHUNKS):
        from_rows(m, slots.at[m], got.at[m])
        a = dot(weights_t[...], got[m])
        x_sends.append(
            exchange(
                0,
                m,
                a[:BEAMS, :128] - a[BEAMS:, 128:],
                a[:BEAMS, 128:] + a[BEAMS:, :128],
                g,
                sibling,
            )
        )
        arrive(0, m, g, sibling)
        real, imag = merge(0, m, bank_perm)
        x_sends.append(exchange(1, m, real, imag, v, partner))
    for m in range(CHUNKS):
        arrive(1, m, v, partner)
        real, imag = merge(1, m, bank_nat)
        outf[pl.ds(2 * m, BEAMS, stride=4), :] = real
        outf[pl.ds(2 * m + 1, BEAMS, stride=4), :] = imag
    out[...] = outf[...].astype(BF16)

    for c1 in first_sends + z_sends + row_sends + x_sends:
        c1.wait_send()


def body(
    raw_samples,
    window,
    steering,
    assignment,
    beam_map,
    interp_index,
    phase_offset,
    phase_rate,
    interp_bank,
):
    dma = pltpu.SemaphoreType.DMA
    vmem = pltpu.VMEM
    out = pl.pallas_call(
        kernel,
        out_shape=pltpu.VMEM((4 * BEAMS, 128), BF16),
        in_specs=[pl.BlockSpec(memory_space=pltpu.HBM)] * 9,
        out_specs=pl.BlockSpec(memory_space=pltpu.VMEM),
        scratch_shapes=[
            vmem((2, P_DEV, NS), BF16),
            vmem((1, NS), F32),
            vmem((2 * P_DEV, BEAMS), BF16),
            vmem((1, P_DEV), I32),
            vmem((4, BEAMS), I32),
            vmem((4, BEAMS), I32),
            vmem((4, BEAMS), F32),
            vmem((4, BEAMS), F32),
            vmem((Q * RT, RT), BF16),
            vmem((8 * P_DEV, 512), BF16),
            vmem((CHUNKS, 512, 256), BF16),
            vmem((2, 8, 256), F32),
            vmem((2, P_DEV, BEAMS), BF16),
            vmem((COLS * P_DEV, BEAMS), BF16),
            vmem((1, 128), F32),
            vmem((COLS, 1, 128), F32),
            vmem((CHUNKS, COLS, P_DEV, 256), BF16),
            vmem((CHUNKS, COLS * P_DEV, 256), BF16),
            vmem((ROWS * SLOTS, 256), BF16),
            vmem((CHUNKS, ROWS * SLOTS, 256), BF16),
            vmem((CHUNKS, ROWS * SLOTS, 256), BF16),
            vmem((ROWS * SLOTS, BEAMS), BF16),
            vmem((2, ROWS * SLOTS, BEAMS), BF16),
            vmem((256, ROWS * SLOTS), BF16),
            vmem((128, 128), F32),
            vmem((RT, Q * RT), BF16),
            vmem((RT, Q * RT), BF16),
            vmem((4, BEAMS, Q * HALF), BF16),
            vmem((4, BEAMS, 256), F32),
            vmem((4, BEAMS, 256), F32),
            vmem((2, CHUNKS, BEAMS, 256), BF16),
            vmem((2, CHUNKS, 2, HALF, 256), BF16),
            vmem((2, Q * HALF, 256), BF16),
            vmem((4 * BEAMS, 128), F32),
            dma((9,)),
            dma((COLS,)),
            dma((COLS,)),
            dma((COLS,)),
            dma((COLS,)),
            dma((CHUNKS, COLS)),
            dma((CHUNKS, COLS)),
            dma((3, ROWS)),
            dma((3, ROWS)),
            dma((4,)),
            dma((4,)),
            dma((2, CHUNKS)),
            dma((2, CHUNKS)),
        ],
        compiler_params=pltpu.CompilerParams(
            collective_id=0, has_side_effects=True, vmem_limit_bytes=56 << 20
        ),
        name="backprojection",
    )(
        raw_samples,
        window.reshape(1, NS),
        steering.reshape(2 * P_DEV, BEAMS),
        assignment.reshape(1, P_DEV),
        beam_map.reshape(4, BEAMS),
        interp_index.reshape(4, BEAMS),
        phase_offset.reshape(4, BEAMS),
        phase_rate.reshape(4, BEAMS),
        interp_bank.reshape(Q * RT, RT),
    )
    out = out.reshape(BEAMS, CHUNKS, 2, RT).transpose(0, 2, 1, 3)
    return out.reshape(1, 1, BEAMS, 2, CHUNKS * RT)


def solution(mesh):
    in_specs = (
        P(None, ("grp", "row", "col"), None),
        P(),
        P(("grp", "row", "col"), None, None),
        P(("grp", "row", "col"), None),
        P(None, "grp", "row", None, None),
        P(None, "grp", "row", None, None),
        P(None, "grp", "row", None, None),
        P(None, "grp", "row", None, None),
        P(),
    )
    out_specs = P("grp", "row", None, None, "col")
    return jax.shard_map(body, mesh=mesh, in_specs=in_specs, out_specs=out_specs, check_vma=False)
```

```python
import math

import jax
import jax.numpy as jnp
from jax import lax
from jax.experimental import pallas as pl
from jax.experimental.pallas import tpu as pltpu
from jax.sharding import PartitionSpec as P

MESH = pl.DeviceIdType.MESH
F32, BF16, I32 = jnp.float32, jnp.bfloat16, jnp.int32

NS = 2048
BEAMS = 128
RT = 128
Q = 8
P_DEV = 32
CAP = 6
ROWS = 16
COLS = 8
SLOTS = COLS * CAP
HALF = BEAMS // 2
CHUNKS = 2

COS = (
    0.9999999890590227,
    -19.73920449945391,
    64.93911745989556,
    -85.45013953088247,
    60.16763095094928,
    -25.967599248494622,
    6.528658161366808,
)
SIN = (
    6.283185302511503,
    -41.341700405317496,
    81.60513138579344,
    -76.70301535379849,
    42.025926985567956,
    -14.89984666736486,
    3.238137509743233,
)


def horner(coefs, y):
    total = jnp.full_like(y, coefs[-1])
    for c in coefs[-2::-1]:
        total = total * y + c
    return total


def cos_sin(turns):
    r = turns - jnp.floor(turns + 0.5)
    y = r * r
    return horner(COS, y), horner(SIN, y) * r


def dft8(xr, xi):
    h = math.sqrt(0.5)
    ur = [xr[j] + xr[j + 4] for j in range(4)]
    ui = [xi[j] + xi[j + 4] for j in range(4)]
    vr = [xr[j] - xr[j + 4] for j in range(4)]
    vi = [xi[j] - xi[j + 4] for j in range(4)]
    wr = [vr[0], (vr[1] + vi[1]) * h, vi[2], (vi[3] - vr[3]) * h]
    wi = [vi[0], (vi[1] - vr[1]) * h, -vr[2], (-vr[3] - vi[3]) * h]
    yr, yi = [None] * 8, [None] * 8
    for odd, (zr, zi) in enumerate(((ur, ui), (wr, wi))):
        ar, ai = zr[0] + zr[2], zi[0] + zi[2]
        br, bi = zr[0] - zr[2], zi[0] - zi[2]
        cr, ci = zr[1] + zr[3], zi[1] + zi[3]
        dr, di = zr[1] - zr[3], zi[1] - zi[3]
        yr[odd], yi[odd] = ar + cr, ai + ci
        yr[odd + 4], yi[odd + 4] = ar - cr, ai - ci
        yr[odd + 2], yi[odd + 2] = br + di, bi - dr
        yr[odd + 6], yi[odd + 6] = br - di, bi + dr
    return yr, yi


def swap_groups(tiles):
    lane = lax.broadcasted_iota(I32, tiles[0].shape, 1)
    tiles = list(tiles)
    for bit in range(3):
        step = 1 << bit
        upper = (lane & (16 * step)) != 0
        for a in range(8):
            if a & step:
                continue
            low, high = tiles[a], tiles[a + step]
            tiles[a] = jnp.where(upper, pltpu.roll(high, 16 * step, 1), low)
            tiles[a + step] = jnp.where(upper, high, pltpu.roll(low, 128 - 16 * step, 1))
    return tiles


def dot(a, b):
    return jnp.dot(a, b, preferred_element_type=F32)


def iota(shape, dim):
    return lax.broadcasted_iota(I32, shape, dim)


def kernel(
    raw_in,
    window_in,
    steering_in,
    assignment_in,
    beam_map_in,
    interp_index_in,
    phase_offset_in,
    phase_rate_in,
    bank_in,
    out,
    raw,
    window,
    steering,
    assignment,
    beam_map,
    interp_index,
    phase_offset,
    phase_rate,
    bank,
    ybuf,
    table,
    twiddle,
    st_own,
    st_all,
    code_own,
    code_all,
    dsend,
    zall,
    sel,
    slots,
    got,
    w_slots,
    w_got,
    weights_t,
    par,
    bank_nat,
    bank_perm,
    picks,
    cosb,
    sinb,
    img,
    child,
    vbuf,
    outf,
    in_sems,
    st_send,
    st_recv,
    code_send,
    code_recv,
    z_send,
    z_recv,
    r_send,
    r_recv,
    p_send,
    p_recv,
    x_send,
    x_recv,
):
    g, row, col = lax.axis_index("grp"), lax.axis_index("row"), lax.axis_index("col")
    ry, rx = row // 4, row % 4

    def remote(src, dst, ssem, rsem, device):
        return pltpu.make_async_remote_copy(
            src_ref=src,
            dst_ref=dst,
            send_sem=ssem,
            recv_sem=rsem,
            device_id=device,
            device_id_type=MESH,
        )

    loads = [
        pltpu.make_async_copy(src, dst, in_sems.at[i])
        for i, (src, dst) in enumerate(
            (
                (assignment_in, assignment),
                (steering_in, steering),
                (window_in, window),
                (raw_in, raw),
                (beam_map_in, beam_map),
                (interp_index_in, interp_index),
                (phase_offset_in, phase_offset),
                (phase_rate_in, phase_rate),
                (bank_in, bank),
            )
        )
    ]
    for load in loads:
        load.start()

    barrier = pltpu.get_barrier_semaphore()

    def greet_col(i, _):
        pl.semaphore_signal(
            barrier, inc=1, device_id=(g, row, (col + i) % COLS), device_id_type=MESH
        )
        return 0

    def greet_row(i, _):
        pl.semaphore_signal(
            barrier, inc=1, device_id=(g, (row + i) % ROWS, col), device_id_type=MESH
        )
        return 0

    lax.fori_loop(1, COLS, greet_col, 0)
    lax.fori_loop(1, ROWS, greet_row, 0)
    pl.semaphore_signal(barrier, inc=1, device_id=(1 - g, row, col), device_id_type=MESH)

    steps = (iota((8, 256), 0) * iota((8, 256), 1)).astype(F32) * (1.0 / NS)
    tc, ts = cos_sin(steps)
    twiddle[0] = tc
    twiddle[1] = ts
    sample = iota((256, 128), 0).astype(F32)
    lane = iota((1, 128), 1)
    for m in range(CHUNKS):
        d = ((lane >> 4) * 32 + (16 * m) + (lane & 15)).astype(F32) * (1.0 / 256)
        c, s = cos_sin(sample * d)
        c, s = c.astype(BF16), s.astype(BF16)
        table[m, :256, :128] = c
        table[m, :256, 128:] = -s
        table[m, 256:, :128] = s
        table[m, 256:, 128:] = c

    loads[0].wait()
    own_row = assignment[...].astype(F32)
    eye = iota((P_DEV, P_DEV), 0) == iota((P_DEV, P_DEV), 1)
    before = iota((P_DEV, P_DEV), 1) < iota((P_DEV, P_DEV), 0)
    own_col = jnp.sum(jnp.where(eye, own_row, 0.0), axis=1, keepdims=True)
    rank = jnp.sum(
        jnp.where(before & (own_col == own_row), 1.0, 0.0), axis=1, keepdims=True
    )
    code_col = own_col * SLOTS + rank + (col * CAP).astype(F32)
    place = iota((P_DEV, 128), 0) + 32 * (col % 4)
    code = jnp.sum(
        jnp.where(iota((P_DEV, 128), 1) == place, code_col, 0.0), axis=0, keepdims=True
    )
    code_own[...] = code

    loads[1].wait()
    pick = iota((2 * P_DEV, 2 * P_DEV), 0)
    pick = (pick % P_DEV) * 2 + pick // P_DEV == iota((2 * P_DEV, 2 * P_DEV), 1)
    parts = dot(pick.astype(F32).astype(BF16), steering[...]).astype(BF16)
    st_own[0] = parts[:P_DEV]
    st_own[1] = parts[P_DEV:]

    pl.semaphore_wait(barrier, COLS - 1 + ROWS - 1 + 1)

    parity = col % 2
    first_sends = []
    for i in (4, 3, 5, 2, 6, 1, 7):
        dest = (col + i) % COLS
        device = (g, row, dest)
        mine = pl.ds(pl.multiple_of(col * P_DEV, P_DEV), P_DEV)
        c1 = remote(code_own, code_all.at[col], code_send.at[i], code_recv.at[col], device)
        c2 = remote(st_own.at[dest % 2], st_all.at[mine], st_send.at[i], st_recv.at[col], device)
        c1.start()
        c2.start()
        first_sends += [c1, c2]
    code_all[col] = code_own[...]
    st_all[pl.ds(pl.multiple_of(col * P_DEV, P_DEV), P_DEV), :] = st_own[parity]

    loads[2].wait()
    loads[3].wait()
    scale = 1.0 / math.sqrt(NS)
    for lh in range(2):
        lanes = [pl.ds(256 * t + 128 * lh, 128) for t in range(8)]
        taper = [window[:, lanes[t]] * scale for t in range(8)]
        for pg in range(P_DEV // 16):
            rows = pl.ds(16 * pg, 16)
            xr = [raw[0, rows, lanes[t]].astype(F32) * taper[t] for t in range(8)]
            xi = [raw[1, rows, lanes[t]].astype(F32) * taper[t] for t in range(8)]
            yr, yi = dft8(xr, xi)
            for c in range(8):
                zr, zi = yr[c], yi[c]
                if c:
                    wc = twiddle[0, c : c + 1, 128 * lh : 128 * lh + 128]
                    ws = twiddle[1, c : c + 1, 128 * lh : 128 * lh + 128]
                    zr, zi = zr * wc + zi * ws, zi * wc - zr * ws
                to = pl.ds(P_DEV * c + 16 * pg, 16)
                ybuf[to, 128 * lh : 128 * lh + 128] = zr.astype(BF16)
                ybuf[to, 256 + 128 * lh : 256 + 128 * lh + 128] = zi.astype(BF16)

    z_sends = []
    for m in range(CHUNKS):
        spectrum = dot(ybuf[...], table[m])
        for part in range(2):
            tiles = swap_groups(
                [
                    spectrum[P_DEV * c : P_DEV * c + P_DEV, 128 * part : 128 * part + 128]
                    for c in range(8)
                ]
            )
            for c in range(8):
                dsend[m, c, :, 128 * part : 128 * part + 128] = tiles[c].astype(BF16)

    def to_cols(m):
        mine = pl.ds(pl.multiple_of(col * P_DEV, P_DEV), P_DEV)
        for i in (1, 4, 7, 3, 5, 2, 6):
            dest = (col + i) % COLS
            c1 = remote(
                dsend.at[m, dest],
                zall.at[m, mine],
                z_send.at[m, i],
                z_recv.at[m, col],
                (g, row, dest),
            )
            c1.start()
            z_sends.append(c1)
        zall[m, mine, :] = dsend[m, col]

    to_cols(0)
    to_cols(1)

    def from_cols(wait):
        for i in range(1, COLS):
            wait((col + i) % COLS)

    def wait_first(source):
        at = pl.ds(pl.multiple_of(source * P_DEV, P_DEV), P_DEV)
        remote(
            code_own, code_all.at[source], code_send.at[0], code_recv.at[source], (g, row, source)
        ).wait_recv()
        remote(
            st_own.at[0], st_all.at[at], st_send.at[0], st_recv.at[source], (g, row, source)
        ).wait_recv()

    from_cols(wait_first)
    low = code_all[0] + code_all[1] + code_all[2] + code_all[3]
    high = code_all[4] + code_all[5] + code_all[6] + code_all[7]
    codes = jnp.concatenate([low, high], axis=1).astype(I32)
    for y in range(4):
        sel[192 * y : 192 * y + 192] = jnp.where(
            iota((192, 256), 0) + 192 * y == codes, 1.0, 0.0
        ).astype(BF16)

    row_sends = []

    def to_owners(kind, data, packed, landed):
        mine = pl.ds(pl.multiple_of(row * SLOTS, SLOTS), SLOTS)
        for dy in (2, 1, 3, 0):
            y = (ry + dy) % 4
            block = pl.ds(pl.multiple_of(y * 4 * SLOTS, 4 * SLOTS), 4 * SLOTS)
            packed[block, :] = dot(sel[block, :], data[...]).astype(BF16)
            for dx in (0, 2, 1, 3):
                dest = y * 4 + (rx + dx) % 4
                there = pl.ds(pl.multiple_of(dest * SLOTS, SLOTS), SLOTS)
                if dy == 0 and dx == 0:
                    landed[mine, :] = packed[mine, :]
                    continue
                c1 = remote(
                    packed.at[there],
                    landed.at[mine],
                    r_send.at[kind, 4 * dy + dx],
                    r_recv.at[kind, row],
                    (g, dest, col),
                )
                c1.start()
                row_sends.append(c1)

    def from_rows(kind, packed, landed, dys=(2, 1, 3, 0)):
        for dy in dys:
            for dx in (0, 2, 1, 3):
                if dy == 0 and dx == 0:
                    continue
                source = (ry - dy + 4) % 4 * 4 + (rx - dx + 4) % 4
                at = pl.ds(pl.multiple_of(source * SLOTS, SLOTS), SLOTS)
                remote(
                    packed.at[at],
                    landed.at[at],
                    r_send.at[kind, 0],
                    r_recv.at[kind, source],
                    (g, source, col),
                ).wait_recv()

    def col_pass(i, part):
        y = (ry - i + 4) % 4
        block = pl.ds(pl.multiple_of(y * 4 * SLOTS, 4 * SLOTS), 4 * SLOTS)
        return remote(
            w_got.at[part, block],
            w_got.at[part, block],
            p_send.at[i],
            p_recv.at[i],
            (g, row, col + 1 - 2 * parity),
        )

    to_owners(2, st_all, w_slots, w_got.at[parity])

    for m in range(CHUNKS):

        def wait_z(source):
            at = pl.ds(pl.multiple_of(source * P_DEV, P_DEV), P_DEV)
            remote(
                dsend.at[m, 0],
                zall.at[m, at],
                z_send.at[m, 0],
                z_recv.at[m, source],
                (g, row, source),
            ).wait_recv()

        from_cols(wait_z)
        to_owners(m, zall.at[m], slots.at[m], got.at[m])

    for dy in (2, 1, 3, 0):
        from_rows(2, w_slots, w_got.at[parity], (dy,))
        c1 = col_pass(dy, parity)
        c1.start()
        row_sends.append(c1)

    for load in loads[4:]:
        load.wait()
    par[...] = jnp.zeros_like(par)
    par[0:4, :] = (interp_index[...] * HALF + beam_map[...]).astype(F32)
    par[8:12, :] = phase_offset[...]
    par[16:20, :] = phase_rate[...]
    columns = par[...].T
    bins = (col * 256 + iota((1, 256), 1)).astype(F32) * (1.0 / NS)
    for ls in range(4):
        code = columns[:, ls : ls + 1].astype(I32)
        picks[ls] = jnp.where(iota((BEAMS, Q * HALF), 1) == code, 1.0, 0.0).astype(BF16)
        angle = columns[:, 8 + ls : 9 + ls] + columns[:, 16 + ls : 17 + ls] * bins
        c, s = cos_sin(angle * (0.5 / math.pi))
        cosb[ls] = c
        sinb[ls] = s
    for q in range(Q):
        bank_nat[:, RT * q : RT * q + RT] = bank[RT * q : RT * q + RT, :]
    lane = iota((RT, RT), 0)
    order = ((lane % 16) * 8 + lane // 16 == iota((RT, RT), 1)).astype(F32).astype(BF16)
    bank_perm[...] = dot(order, bank_nat[...]).astype(BF16)

    for dy in (2, 1, 3, 0):
        col_pass(dy, 1 - parity).wait_recv()
    weights_t[:BEAMS] = w_got[0].T
    weights_t[BEAMS:] = w_got[1].T

    def half(bit):
        return pl.ds(pl.multiple_of(bit * HALF, HALF), HALF)

    def interpolated(level, m, child_of, matrices, slot):
        both = child[level, m, child_of]
        v = dot(
            jnp.concatenate([both[:, :128], both[:, 128:]], axis=0), matrices[...]
        ).astype(BF16)
        for part in range(2):
            for q in range(Q):
                vbuf[slot, HALF * q : HALF * q + HALF, 128 * part : 128 * part + 128] = v[
                    HALF * part : HALF * part + HALF, RT * q : RT * q + RT
                ]

    def term(level, m, child_of, slot, beams):
        t = dot(picks[2 * level + child_of, beams, :], vbuf[slot])
        tr, ti = t[:, :128], t[:, 128:]
        c = cosb[2 * level + child_of, beams, 128 * m : 128 * m + 128]
        d = sinb[2 * level + child_of, beams, 128 * m : 128 * m + 128]
        return tr * c - ti * d, tr * d + ti * c

    def send(level, m, real, imag, bit, device):
        img[level, m, :, :128] = real.astype(BF16)
        img[level, m, :, 128:] = imag.astype(BF16)
        c1 = remote(
            img.at[level, m],
            child.at[level, m, bit],
            x_send.at[level, m],
            x_recv.at[level, m],
            device,
        )
        c1.start()
        x_sends.append(c1)

    def keep(level, m, real, imag, bit):
        child[level, m, bit, :, :128] = real.astype(BF16)
        child[level, m, bit, :, 128:] = imag.astype(BF16)

    def arrive(level, m, bit, device):
        remote(
            img.at[level, m],
            child.at[level, m, 1 - bit],
            x_send.at[level, m],
            x_recv.at[level, m],
            device,
        ).wait_recv()

    def beams_of(m, bit):
        lhs = jnp.concatenate(
            [weights_t[half(bit), :], weights_t[half(bit + 2), :]], axis=0
        )
        a = dot(lhs, got[m])
        return a[:HALF, :128] - a[HALF:, 128:], a[:HALF, 128:] + a[HALF:, :128]

    sibling = (1 - g, row, col)
    v = row % 2
    partner = (g, row + 1 - 2 * v, col)
    every = slice(None)
    x_sends = []
    for m in range(CHUNKS):
        from_rows(m, slots.at[m], got.at[m])
        send(0, m, *beams_of(m, 1 - g), g, sibling)
        keep(0, m, *beams_of(m, g), g)
        interpolated(0, m, g, bank_perm, 0)
        give_r, give_i = term(0, m, g, 0, half(1 - v))
        keep_r, keep_i = term(0, m, g, 0, half(v))
        arrive(0, m, g, sibling)
        interpolated(0, m, 1 - g, bank_perm, 1)
        r, i = term(0, m, 1 - g, 1, half(1 - v))
        send(1, m, give_r + r, give_i + i, v, partner)
        r, i = term(0, m, 1 - g, 1, half(v))
        keep(1, m, keep_r + r, keep_i + i, v)
    for m in range(CHUNKS):
        interpolated(1, m, v, bank_nat, 0)
        own_r, own_i = term(1, m, v, 0, every)
        arrive(1, m, v, partner)
        interpolated(1, m, 1 - v, bank_nat, 1)
        r, i = term(1, m, 1 - v, 1, every)
        outf[pl.ds(2 * m, BEAMS, stride=4), :] = own_r + r
        outf[pl.ds(2 * m + 1, BEAMS, stride=4), :] = own_i + i
    out[...] = outf[...].astype(BF16)

    for c1 in first_sends + z_sends + row_sends + x_sends:
        c1.wait_send()


def body(
    raw_samples,
    window,
    steering,
    assignment,
    beam_map,
    interp_index,
    phase_offset,
    phase_rate,
    interp_bank,
):
    dma = pltpu.SemaphoreType.DMA
    vmem = pltpu.VMEM
    out = pl.pallas_call(
        kernel,
        out_shape=pltpu.VMEM((4 * BEAMS, 128), BF16),
        in_specs=[pl.BlockSpec(memory_space=pltpu.HBM)] * 9,
        out_specs=pl.BlockSpec(memory_space=pltpu.VMEM),
        scratch_shapes=[
            vmem((2, P_DEV, NS), BF16),
            vmem((1, NS), F32),
            vmem((2 * P_DEV, BEAMS), BF16),
            vmem((1, P_DEV), I32),
            vmem((4, BEAMS), I32),
            vmem((4, BEAMS), I32),
            vmem((4, BEAMS), F32),
            vmem((4, BEAMS), F32),
            vmem((Q * RT, RT), BF16),
            vmem((8 * P_DEV, 512), BF16),
            vmem((CHUNKS, 512, 256), BF16),
            vmem((2, 8, 256), F32),
            vmem((2, P_DEV, BEAMS), BF16),
            vmem((COLS * P_DEV, BEAMS), BF16),
            vmem((1, 128), F32),
            vmem((COLS, 1, 128), F32),
            vmem((CHUNKS, COLS, P_DEV, 256), BF16),
            vmem((CHUNKS, COLS * P_DEV, 256), BF16),
            vmem((ROWS * SLOTS, 256), BF16),
            vmem((CHUNKS, ROWS * SLOTS, 256), BF16),
            vmem((CHUNKS, ROWS * SLOTS, 256), BF16),
            vmem((ROWS * SLOTS, BEAMS), BF16),
            vmem((2, ROWS * SLOTS, BEAMS), BF16),
            vmem((256, ROWS * SLOTS), BF16),
            vmem((128, 128), F32),
            vmem((RT, Q * RT), BF16),
            vmem((RT, Q * RT), BF16),
            vmem((4, BEAMS, Q * HALF), BF16),
            vmem((4, BEAMS, 256), F32),
            vmem((4, BEAMS, 256), F32),
            vmem((2, CHUNKS, HALF, 256), BF16),
            vmem((2, CHUNKS, 2, HALF, 256), BF16),
            vmem((2, Q * HALF, 256), BF16),
            vmem((4 * BEAMS, 128), F32),
            dma((9,)),
            dma((COLS,)),
            dma((COLS,)),
            dma((COLS,)),
            dma((COLS,)),
            dma((CHUNKS, COLS)),
            dma((CHUNKS, COLS)),
            dma((3, ROWS)),
            dma((3, ROWS)),
            dma((4,)),
            dma((4,)),
            dma((2, CHUNKS)),
            dma((2, CHUNKS)),
        ],
        compiler_params=pltpu.CompilerParams(
            collective_id=0, has_side_effects=True, vmem_limit_bytes=56 << 20
        ),
        name="backprojection",
    )(
        raw_samples,
        window.reshape(1, NS),
        steering.reshape(2 * P_DEV, BEAMS),
        assignment.reshape(1, P_DEV),
        beam_map.reshape(4, BEAMS),
        interp_index.reshape(4, BEAMS),
        phase_offset.reshape(4, BEAMS),
        phase_rate.reshape(4, BEAMS),
        interp_bank.reshape(Q * RT, RT),
    )
    out = out.reshape(BEAMS, CHUNKS, 2, RT).transpose(0, 2, 1, 3)
    return out.reshape(1, 1, BEAMS, 2, CHUNKS * RT)


def solution(mesh):
    in_specs = (
        P(None, ("grp", "row", "col"), None),
        P(),
        P(("grp", "row", "col"), None, None),
        P(("grp", "row", "col"), None),
        P(None, "grp", "row", None, None),
        P(None, "grp", "row", None, None),
        P(None, "grp", "row", None, None),
        P(None, "grp", "row", None, None),
        P(),
    )
    out_specs = P("grp", "row", None, None, "col")
    return jax.shard_map(body, mesh=mesh, in_specs=in_specs, out_specs=out_specs, check_vma=False)
```

```python
import math

import jax
import jax.numpy as jnp
from jax import lax
from jax.experimental import pallas as pl
from jax.experimental.pallas import tpu as pltpu
from jax.sharding import PartitionSpec as P

MESH = pl.DeviceIdType.MESH
F32, BF16, I32 = jnp.float32, jnp.bfloat16, jnp.int32

NS = 2048
BEAMS = 128
RT = 128
Q = 8
P_DEV = 32
CAP = 6
ROWS = 16
COLS = 8
SLOTS = COLS * CAP
HALF = BEAMS // 2
CHUNKS = 2

COS = (
    0.9999999890590227,
    -19.73920449945391,
    64.93911745989556,
    -85.45013953088247,
    60.16763095094928,
    -25.967599248494622,
    6.528658161366808,
)
SIN = (
    6.283185302511503,
    -41.341700405317496,
    81.60513138579344,
    -76.70301535379849,
    42.025926985567956,
    -14.89984666736486,
    3.238137509743233,
)


def horner(coefs, y):
    total = jnp.full_like(y, coefs[-1])
    for c in coefs[-2::-1]:
        total = total * y + c
    return total


def cos_sin(turns):
    r = turns - jnp.floor(turns + 0.5)
    y = r * r
    return horner(COS, y), horner(SIN, y) * r


def dft8(xr, xi):
    h = math.sqrt(0.5)
    ur = [xr[j] + xr[j + 4] for j in range(4)]
    ui = [xi[j] + xi[j + 4] for j in range(4)]
    vr = [xr[j] - xr[j + 4] for j in range(4)]
    vi = [xi[j] - xi[j + 4] for j in range(4)]
    wr = [vr[0], (vr[1] + vi[1]) * h, vi[2], (vi[3] - vr[3]) * h]
    wi = [vi[0], (vi[1] - vr[1]) * h, -vr[2], (-vr[3] - vi[3]) * h]
    yr, yi = [None] * 8, [None] * 8
    for odd, (zr, zi) in enumerate(((ur, ui), (wr, wi))):
        ar, ai = zr[0] + zr[2], zi[0] + zi[2]
        br, bi = zr[0] - zr[2], zi[0] - zi[2]
        cr, ci = zr[1] + zr[3], zi[1] + zi[3]
        dr, di = zr[1] - zr[3], zi[1] - zi[3]
        yr[odd], yi[odd] = ar + cr, ai + ci
        yr[odd + 4], yi[odd + 4] = ar - cr, ai - ci
        yr[odd + 2], yi[odd + 2] = br + di, bi - dr
        yr[odd + 6], yi[odd + 6] = br - di, bi + dr
    return yr, yi


def swap_groups(tiles):
    lane = lax.broadcasted_iota(I32, tiles[0].shape, 1)
    tiles = list(tiles)
    for bit in range(3):
        step = 1 << bit
        upper = (lane & (16 * step)) != 0
        for a in range(8):
            if a & step:
                continue
            low, high = tiles[a], tiles[a + step]
            tiles[a] = jnp.where(upper, pltpu.roll(high, 16 * step, 1), low)
            tiles[a + step] = jnp.where(upper, high, pltpu.roll(low, 128 - 16 * step, 1))
    return tiles


def dot(a, b):
    return jnp.dot(a, b, preferred_element_type=F32)


def iota(shape, dim):
    return lax.broadcasted_iota(I32, shape, dim)


def kernel(
    raw_in,
    window_in,
    steering_in,
    assignment_in,
    beam_map_in,
    interp_index_in,
    phase_offset_in,
    phase_rate_in,
    bank_in,
    out,
    raw,
    window,
    steering,
    assignment,
    beam_map,
    interp_index,
    phase_offset,
    phase_rate,
    bank,
    ybuf,
    table,
    twiddle,
    st_own,
    st_all,
    code_own,
    code_all,
    dsend,
    zall,
    sel,
    slots,
    got,
    w_slots,
    w_got,
    weights_t,
    par,
    bank_nat,
    bank_perm,
    picks,
    cosb,
    sinb,
    img,
    child,
    vbuf,
    outf,
    in_sems,
    st_send,
    st_recv,
    code_send,
    code_recv,
    z_send,
    z_recv,
    r_send,
    r_recv,
    p_send,
    p_recv,
    x_send,
    x_recv,
):
    g, row, col = lax.axis_index("grp"), lax.axis_index("row"), lax.axis_index("col")
    ry, rx = row // 4, row % 4

    def remote(src, dst, ssem, rsem, device):
        return pltpu.make_async_remote_copy(
            src_ref=src,
            dst_ref=dst,
            send_sem=ssem,
            recv_sem=rsem,
            device_id=device,
            device_id_type=MESH,
        )

    loads = [
        pltpu.make_async_copy(src, dst, in_sems.at[i])
        for i, (src, dst) in enumerate(
            (
                (assignment_in, assignment),
                (steering_in, steering),
                (window_in, window),
                (raw_in, raw),
                (beam_map_in, beam_map),
                (interp_index_in, interp_index),
                (phase_offset_in, phase_offset),
                (phase_rate_in, phase_rate),
                (bank_in, bank),
            )
        )
    ]
    for load in loads:
        load.start()

    barrier = pltpu.get_barrier_semaphore()

    def greet_col(i, _):
        pl.semaphore_signal(
            barrier, inc=1, device_id=(g, row, (col + i) % COLS), device_id_type=MESH
        )
        return 0

    def greet_row(i, _):
        pl.semaphore_signal(
            barrier, inc=1, device_id=(g, (row + i) % ROWS, col), device_id_type=MESH
        )
        return 0

    lax.fori_loop(1, COLS, greet_col, 0)
    lax.fori_loop(1, ROWS, greet_row, 0)
    pl.semaphore_signal(barrier, inc=1, device_id=(1 - g, row, col), device_id_type=MESH)

    steps = (iota((8, 256), 0) * iota((8, 256), 1)).astype(F32) * (1.0 / NS)
    tc, ts = cos_sin(steps)
    twiddle[0] = tc
    twiddle[1] = ts
    sample = iota((256, 128), 0).astype(F32)
    lane = iota((1, 128), 1)
    for m in range(CHUNKS):
        d = ((lane >> 4) * 32 + (16 * m) + (lane & 15)).astype(F32) * (1.0 / 256)
        c, s = cos_sin(sample * d)
        c, s = c.astype(BF16), s.astype(BF16)
        table[m, :256, :128] = c
        table[m, :256, 128:] = -s
        table[m, 256:, :128] = s
        table[m, 256:, 128:] = c

    loads[0].wait()
    own_row = assignment[...].astype(F32)
    eye = iota((P_DEV, P_DEV), 0) == iota((P_DEV, P_DEV), 1)
    before = iota((P_DEV, P_DEV), 1) < iota((P_DEV, P_DEV), 0)
    own_col = jnp.sum(jnp.where(eye, own_row, 0.0), axis=1, keepdims=True)
    rank = jnp.sum(
        jnp.where(before & (own_col == own_row), 1.0, 0.0), axis=1, keepdims=True
    )
    code_col = own_col * SLOTS + rank + (col * CAP).astype(F32)
    place = iota((P_DEV, 128), 0) + 32 * (col % 4)
    code = jnp.sum(
        jnp.where(iota((P_DEV, 128), 1) == place, code_col, 0.0), axis=0, keepdims=True
    )
    code_own[...] = code

    loads[1].wait()
    pick = iota((2 * P_DEV, 2 * P_DEV), 0)
    pick = (pick % P_DEV) * 2 + pick // P_DEV == iota((2 * P_DEV, 2 * P_DEV), 1)
    parts = dot(pick.astype(F32).astype(BF16), steering[...]).astype(BF16)
    st_own[0] = parts[:P_DEV]
    st_own[1] = parts[P_DEV:]

    pl.semaphore_wait(barrier, COLS - 1 + ROWS - 1 + 1)

    parity = col % 2
    first_sends = []
    mine = pl.ds(pl.multiple_of(col * P_DEV, P_DEV), P_DEV)
    for i in (4, 3, 5, 2, 6, 1, 7):
        dest = (col + i) % COLS
        c1 = remote(
            code_own, code_all.at[col], code_send.at[i], code_recv.at[col], (g, row, dest)
        )
        c1.start()
        first_sends.append(c1)
    for i in (4, 3, 5, 2, 6, 1, 7):
        dest = (col + i) % COLS
        c1 = remote(
            st_own.at[dest % 2], st_all.at[mine], st_send.at[i], st_recv.at[col], (g, row, dest)
        )
        c1.start()
        first_sends.append(c1)
    code_all[col] = code_own[...]
    st_all[pl.ds(pl.multiple_of(col * P_DEV, P_DEV), P_DEV), :] = st_own[parity]

    loads[2].wait()
    loads[3].wait()
    scale = 1.0 / math.sqrt(NS)
    for lh in range(2):
        lanes = [pl.ds(256 * t + 128 * lh, 128) for t in range(8)]
        taper = [window[:, lanes[t]] * scale for t in range(8)]
        for pg in range(P_DEV // 16):
            rows = pl.ds(16 * pg, 16)
            xr = [raw[0, rows, lanes[t]].astype(F32) * taper[t] for t in range(8)]
            xi = [raw[1, rows, lanes[t]].astype(F32) * taper[t] for t in range(8)]
            yr, yi = dft8(xr, xi)
            for c in range(8):
                zr, zi = yr[c], yi[c]
                if c:
                    wc = twiddle[0, c : c + 1, 128 * lh : 128 * lh + 128]
                    ws = twiddle[1, c : c + 1, 128 * lh : 128 * lh + 128]
                    zr, zi = zr * wc + zi * ws, zi * wc - zr * ws
                to = pl.ds(P_DEV * c + 16 * pg, 16)
                ybuf[to, 128 * lh : 128 * lh + 128] = zr.astype(BF16)
                ybuf[to, 256 + 128 * lh : 256 + 128 * lh + 128] = zi.astype(BF16)

    z_sends = []
    for m in range(CHUNKS):
        spectrum = dot(ybuf[...], table[m])
        for part in range(2):
            tiles = swap_groups(
                [
                    spectrum[P_DEV * c : P_DEV * c + P_DEV, 128 * part : 128 * part + 128]
                    for c in range(8)
                ]
            )
            for c in range(8):
                dsend[m, c, :, 128 * part : 128 * part + 128] = tiles[c].astype(BF16)

    def to_cols(m):
        mine = pl.ds(pl.multiple_of(col * P_DEV, P_DEV), P_DEV)
        for i in (1, 4, 7, 3, 5, 2, 6):
            dest = (col + i) % COLS
            c1 = remote(
                dsend.at[m, dest],
                zall.at[m, mine],
                z_send.at[m, i],
                z_recv.at[m, col],
                (g, row, dest),
            )
            c1.start()
            z_sends.append(c1)
        zall[m, mine, :] = dsend[m, col]

    to_cols(0)
    to_cols(1)

    def from_cols(wait):
        for i in range(1, COLS):
            wait((col + i) % COLS)

    def wait_code(source):
        remote(
            code_own, code_all.at[source], code_send.at[0], code_recv.at[source], (g, row, source)
        ).wait_recv()

    def wait_steering(source):
        at = pl.ds(pl.multiple_of(source * P_DEV, P_DEV), P_DEV)
        remote(
            st_own.at[0], st_all.at[at], st_send.at[0], st_recv.at[source], (g, row, source)
        ).wait_recv()

    from_cols(wait_code)
    low = code_all[0] + code_all[1] + code_all[2] + code_all[3]
    high = code_all[4] + code_all[5] + code_all[6] + code_all[7]
    codes = jnp.concatenate([low, high], axis=1).astype(I32)
    for y in range(4):
        sel[192 * y : 192 * y + 192] = jnp.where(
            iota((192, 256), 0) + 192 * y == codes, 1.0, 0.0
        ).astype(BF16)
    from_cols(wait_steering)

    row_sends = []

    def to_owners(kind, data, packed, landed):
        mine = pl.ds(pl.multiple_of(row * SLOTS, SLOTS), SLOTS)
        for dy in (2, 1, 3, 0):
            y = (ry + dy) % 4
            block = pl.ds(pl.multiple_of(y * 4 * SLOTS, 4 * SLOTS), 4 * SLOTS)
            packed[block, :] = dot(sel[block, :], data[...]).astype(BF16)
            for dx in (0, 2, 1, 3):
                dest = y * 4 + (rx + dx) % 4
                there = pl.ds(pl.multiple_of(dest * SLOTS, SLOTS), SLOTS)
                if dy == 0 and dx == 0:
                    landed[mine, :] = packed[mine, :]
                    continue
                c1 = remote(
                    packed.at[there],
                    landed.at[mine],
                    r_send.at[kind, 4 * dy + dx],
                    r_recv.at[kind, row],
                    (g, dest, col),
                )
                c1.start()
                row_sends.append(c1)

    def from_rows(kind, packed, landed, dys=(2, 1, 3, 0)):
        for dy in dys:
            for dx in (0, 2, 1, 3):
                if dy == 0 and dx == 0:
                    continue
                source = (ry - dy + 4) % 4 * 4 + (rx - dx + 4) % 4
                at = pl.ds(pl.multiple_of(source * SLOTS, SLOTS), SLOTS)
                remote(
                    packed.at[at],
                    landed.at[at],
                    r_send.at[kind, 0],
                    r_recv.at[kind, source],
                    (g, source, col),
                ).wait_recv()

    def col_pass(i, part):
        y = (ry - i + 4) % 4
        block = pl.ds(pl.multiple_of(y * 4 * SLOTS, 4 * SLOTS), 4 * SLOTS)
        return remote(
            w_got.at[part, block],
            w_got.at[part, block],
            p_send.at[i],
            p_recv.at[i],
            (g, row, col + 1 - 2 * parity),
        )

    to_owners(2, st_all, w_slots, w_got.at[parity])

    for m in range(CHUNKS):

        def wait_z(source):
            at = pl.ds(pl.multiple_of(source * P_DEV, P_DEV), P_DEV)
            remote(
                dsend.at[m, 0],
                zall.at[m, at],
                z_send.at[m, 0],
                z_recv.at[m, source],
                (g, row, source),
            ).wait_recv()

        from_cols(wait_z)
        to_owners(m, zall.at[m], slots.at[m], got.at[m])

    for dy in (2, 1, 3, 0):
        from_rows(2, w_slots, w_got.at[parity], (dy,))
        c1 = col_pass(dy, parity)
        c1.start()
        row_sends.append(c1)

    for load in loads[4:]:
        load.wait()
    par[...] = jnp.zeros_like(par)
    par[0:4, :] = (interp_index[...] * HALF + beam_map[...]).astype(F32)
    par[8:12, :] = phase_offset[...]
    par[16:20, :] = phase_rate[...]
    columns = par[...].T
    bins = (col * 256 + iota((1, 256), 1)).astype(F32) * (1.0 / NS)
    for ls in range(4):
        code = columns[:, ls : ls + 1].astype(I32)
        picks[ls] = jnp.where(iota((BEAMS, Q * HALF), 1) == code, 1.0, 0.0).astype(BF16)
        angle = columns[:, 8 + ls : 9 + ls] + columns[:, 16 + ls : 17 + ls] * bins
        c, s = cos_sin(angle * (0.5 / math.pi))
        cosb[ls] = c
        sinb[ls] = s
    for q in range(Q):
        bank_nat[:, RT * q : RT * q + RT] = bank[RT * q : RT * q + RT, :]
    lane = iota((RT, RT), 0)
    order = ((lane % 16) * 8 + lane // 16 == iota((RT, RT), 1)).astype(F32).astype(BF16)
    bank_perm[...] = dot(order, bank_nat[...]).astype(BF16)

    weights_t[pl.ds(pl.multiple_of(parity * BEAMS, BEAMS), BEAMS), :] = w_got[parity].T
    for dy in (2, 1, 3, 0):
        col_pass(dy, 1 - parity).wait_recv()
    weights_t[pl.ds(pl.multiple_of((1 - parity) * BEAMS, BEAMS), BEAMS), :] = w_got[1 - parity].T

    def half(bit):
        return pl.ds(pl.multiple_of(bit * HALF, HALF), HALF)

    def interpolated(level, m, child_of, matrices, slot):
        both = child[level, m, child_of]
        v = dot(
            jnp.concatenate([both[:, :128], both[:, 128:]], axis=0), matrices[...]
        ).astype(BF16)
        for part in range(2):
            for q in range(Q):
                vbuf[slot, HALF * q : HALF * q + HALF, 128 * part : 128 * part + 128] = v[
                    HALF * part : HALF * part + HALF, RT * q : RT * q + RT
                ]

    def term(level, m, child_of, slot, beams):
        t = dot(picks[2 * level + child_of, beams, :], vbuf[slot])
        tr, ti = t[:, :128], t[:, 128:]
        c = cosb[2 * level + child_of, beams, 128 * m : 128 * m + 128]
        d = sinb[2 * level + child_of, beams, 128 * m : 128 * m + 128]
        return tr * c - ti * d, tr * d + ti * c

    def send(level, m, real, imag, bit, device):
        img[level, m, :, :128] = real.astype(BF16)
        img[level, m, :, 128:] = imag.astype(BF16)
        c1 = remote(
            img.at[level, m],
            child.at[level, m, bit],
            x_send.at[level, m],
            x_recv.at[level, m],
            device,
        )
        c1.start()
        x_sends.append(c1)

    def keep(level, m, real, imag, bit):
        child[level, m, bit, :, :128] = real.astype(BF16)
        child[level, m, bit, :, 128:] = imag.astype(BF16)

    def arrive(level, m, bit, device):
        remote(
            img.at[level, m],
            child.at[level, m, 1 - bit],
            x_send.at[level, m],
            x_recv.at[level, m],
            device,
        ).wait_recv()

    def beams_of(m, bit):
        lhs = jnp.concatenate(
            [weights_t[half(bit), :], weights_t[half(bit + 2), :]], axis=0
        )
        a = dot(lhs, got[m])
        return a[:HALF, :128] - a[HALF:, 128:], a[:HALF, 128:] + a[HALF:, :128]

    sibling = (1 - g, row, col)
    v = row % 2
    partner = (g, row + 1 - 2 * v, col)
    every = slice(None)
    x_sends = []
    for m in range(CHUNKS):
        from_rows(m, slots.at[m], got.at[m])
        send(0, m, *beams_of(m, 1 - g), g, sibling)
        keep(0, m, *beams_of(m, g), g)
        interpolated(0, m, g, bank_perm, 0)
        give_r, give_i = term(0, m, g, 0, half(1 - v))
        keep_r, keep_i = term(0, m, g, 0, half(v))
        arrive(0, m, g, sibling)
        interpolated(0, m, 1 - g, bank_perm, 1)
        r, i = term(0, m, 1 - g, 1, half(1 - v))
        send(1, m, give_r + r, give_i + i, v, partner)
        r, i = term(0, m, 1 - g, 1, half(v))
        keep(1, m, keep_r + r, keep_i + i, v)
    for m in range(CHUNKS):
        interpolated(1, m, v, bank_nat, 0)
        own_r, own_i = term(1, m, v, 0, every)
        arrive(1, m, v, partner)
        interpolated(1, m, 1 - v, bank_nat, 1)
        r, i = term(1, m, 1 - v, 1, every)
        outf[pl.ds(2 * m, BEAMS, stride=4), :] = own_r + r
        outf[pl.ds(2 * m + 1, BEAMS, stride=4), :] = own_i + i
    out[...] = outf[...].astype(BF16)

    for c1 in first_sends + z_sends + row_sends + x_sends:
        c1.wait_send()


def body(
    raw_samples,
    window,
    steering,
    assignment,
    beam_map,
    interp_index,
    phase_offset,
    phase_rate,
    interp_bank,
):
    dma = pltpu.SemaphoreType.DMA
    vmem = pltpu.VMEM
    out = pl.pallas_call(
        kernel,
        out_shape=pltpu.VMEM((4 * BEAMS, 128), BF16),
        in_specs=[pl.BlockSpec(memory_space=pltpu.HBM)] * 9,
        out_specs=pl.BlockSpec(memory_space=pltpu.VMEM),
        scratch_shapes=[
            vmem((2, P_DEV, NS), BF16),
            vmem((1, NS), F32),
            vmem((2 * P_DEV, BEAMS), BF16),
            vmem((1, P_DEV), I32),
            vmem((4, BEAMS), I32),
            vmem((4, BEAMS), I32),
            vmem((4, BEAMS), F32),
            vmem((4, BEAMS), F32),
            vmem((Q * RT, RT), BF16),
            vmem((8 * P_DEV, 512), BF16),
            vmem((CHUNKS, 512, 256), BF16),
            vmem((2, 8, 256), F32),
            vmem((2, P_DEV, BEAMS), BF16),
            vmem((COLS * P_DEV, BEAMS), BF16),
            vmem((1, 128), F32),
            vmem((COLS, 1, 128), F32),
            vmem((CHUNKS, COLS, P_DEV, 256), BF16),
            vmem((CHUNKS, COLS * P_DEV, 256), BF16),
            vmem((ROWS * SLOTS, 256), BF16),
            vmem((CHUNKS, ROWS * SLOTS, 256), BF16),
            vmem((CHUNKS, ROWS * SLOTS, 256), BF16),
            vmem((ROWS * SLOTS, BEAMS), BF16),
            vmem((2, ROWS * SLOTS, BEAMS), BF16),
            vmem((256, ROWS * SLOTS), BF16),
            vmem((128, 128), F32),
            vmem((RT, Q * RT), BF16),
            vmem((RT, Q * RT), BF16),
            vmem((4, BEAMS, Q * HALF), BF16),
            vmem((4, BEAMS, 256), F32),
            vmem((4, BEAMS, 256), F32),
            vmem((2, CHUNKS, HALF, 256), BF16),
            vmem((2, CHUNKS, 2, HALF, 256), BF16),
            vmem((2, Q * HALF, 256), BF16),
            vmem((4 * BEAMS, 128), F32),
            dma((9,)),
            dma((COLS,)),
            dma((COLS,)),
            dma((COLS,)),
            dma((COLS,)),
            dma((CHUNKS, COLS)),
            dma((CHUNKS, COLS)),
            dma((3, ROWS)),
            dma((3, ROWS)),
            dma((4,)),
            dma((4,)),
            dma((2, CHUNKS)),
            dma((2, CHUNKS)),
        ],
        compiler_params=pltpu.CompilerParams(
            collective_id=0, has_side_effects=True, vmem_limit_bytes=56 << 20
        ),
        name="backprojection",
    )(
        raw_samples,
        window.reshape(1, NS),
        steering.reshape(2 * P_DEV, BEAMS),
        assignment.reshape(1, P_DEV),
        beam_map.reshape(4, BEAMS),
        interp_index.reshape(4, BEAMS),
        phase_offset.reshape(4, BEAMS),
        phase_rate.reshape(4, BEAMS),
        interp_bank.reshape(Q * RT, RT),
    )
    out = out.reshape(BEAMS, CHUNKS, 2, RT).transpose(0, 2, 1, 3)
    return out.reshape(1, 1, BEAMS, 2, CHUNKS * RT)


def solution(mesh):
    in_specs = (
        P(None, ("grp", "row", "col"), None),
        P(),
        P(("grp", "row", "col"), None, None),
        P(("grp", "row", "col"), None),
        P(None, "grp", "row", None, None),
        P(None, "grp", "row", None, None),
        P(None, "grp", "row", None, None),
        P(None, "grp", "row", None, None),
        P(),
    )
    out_specs = P("grp", "row", None, None, "col")
    return jax.shard_map(body, mesh=mesh, in_specs=in_specs, out_specs=out_specs, check_vma=False)
```

```python
import math

import jax
import jax.numpy as jnp
from jax import lax
from jax.experimental import pallas as pl
from jax.experimental.pallas import tpu as pltpu
from jax.sharding import PartitionSpec as P

MESH = pl.DeviceIdType.MESH
F32, BF16, I32 = jnp.float32, jnp.bfloat16, jnp.int32

NS = 2048
BEAMS = 128
RT = 128
Q = 8
P_DEV = 32
CAP = 6
ROWS = 16
COLS = 8
SLOTS = COLS * CAP
HALF = BEAMS // 2
CHUNKS = 2

COS = (
    0.9999999890590227,
    -19.73920449945391,
    64.93911745989556,
    -85.45013953088247,
    60.16763095094928,
    -25.967599248494622,
    6.528658161366808,
)
SIN = (
    6.283185302511503,
    -41.341700405317496,
    81.60513138579344,
    -76.70301535379849,
    42.025926985567956,
    -14.89984666736486,
    3.238137509743233,
)


def horner(coefs, y):
    total = jnp.full_like(y, coefs[-1])
    for c in coefs[-2::-1]:
        total = total * y + c
    return total


def cos_sin(turns):
    r = turns - jnp.floor(turns + 0.5)
    y = r * r
    return horner(COS, y), horner(SIN, y) * r


def dft8(xr, xi):
    h = math.sqrt(0.5)
    ur = [xr[j] + xr[j + 4] for j in range(4)]
    ui = [xi[j] + xi[j + 4] for j in range(4)]
    vr = [xr[j] - xr[j + 4] for j in range(4)]
    vi = [xi[j] - xi[j + 4] for j in range(4)]
    wr = [vr[0], (vr[1] + vi[1]) * h, vi[2], (vi[3] - vr[3]) * h]
    wi = [vi[0], (vi[1] - vr[1]) * h, -vr[2], (-vr[3] - vi[3]) * h]
    yr, yi = [None] * 8, [None] * 8
    for odd, (zr, zi) in enumerate(((ur, ui), (wr, wi))):
        ar, ai = zr[0] + zr[2], zi[0] + zi[2]
        br, bi = zr[0] - zr[2], zi[0] - zi[2]
        cr, ci = zr[1] + zr[3], zi[1] + zi[3]
        dr, di = zr[1] - zr[3], zi[1] - zi[3]
        yr[odd], yi[odd] = ar + cr, ai + ci
        yr[odd + 4], yi[odd + 4] = ar - cr, ai - ci
        yr[odd + 2], yi[odd + 2] = br + di, bi - dr
        yr[odd + 6], yi[odd + 6] = br - di, bi + dr
    return yr, yi


def swap_groups(tiles):
    lane = lax.broadcasted_iota(I32, tiles[0].shape, 1)
    tiles = list(tiles)
    for bit in range(3):
        step = 1 << bit
        upper = (lane & (16 * step)) != 0
        for a in range(8):
            if a & step:
                continue
            low, high = tiles[a], tiles[a + step]
            tiles[a] = jnp.where(upper, pltpu.roll(high, 16 * step, 1), low)
            tiles[a + step] = jnp.where(upper, high, pltpu.roll(low, 128 - 16 * step, 1))
    return tiles


def dot(a, b):
    return jnp.dot(a, b, preferred_element_type=F32)


def iota(shape, dim):
    return lax.broadcasted_iota(I32, shape, dim)


def kernel(
    raw_in,
    window_in,
    steering_in,
    assignment_in,
    beam_map_in,
    interp_index_in,
    phase_offset_in,
    phase_rate_in,
    bank_in,
    out,
    raw,
    window,
    steering,
    assignment,
    beam_map,
    interp_index,
    phase_offset,
    phase_rate,
    bank,
    ybuf,
    table,
    twiddle,
    st_own,
    st_all,
    code_own,
    code_all,
    dsend,
    zall,
    sel,
    slots,
    got,
    w_slots,
    w_got,
    weights_t,
    par,
    bank_nat,
    bank_perm,
    picks,
    cosb,
    sinb,
    img,
    child,
    vbuf,
    outf,
    in_sems,
    st_send,
    st_recv,
    code_send,
    code_recv,
    z_send,
    z_recv,
    r_send,
    r_recv,
    p_send,
    p_recv,
    x_send,
    x_recv,
):
    g, row, col = lax.axis_index("grp"), lax.axis_index("row"), lax.axis_index("col")
    ry, rx = row // 4, row % 4

    def remote(src, dst, ssem, rsem, device):
        return pltpu.make_async_remote_copy(
            src_ref=src,
            dst_ref=dst,
            send_sem=ssem,
            recv_sem=rsem,
            device_id=device,
            device_id_type=MESH,
        )

    barrier = pltpu.get_barrier_semaphore()

    def greet_col(i, _):
        pl.semaphore_signal(
            barrier, inc=1, device_id=(g, row, (col + i) % COLS), device_id_type=MESH
        )
        return 0

    def greet_row(i, _):
        pl.semaphore_signal(
            barrier, inc=1, device_id=(g, (row + i) % ROWS, col), device_id_type=MESH
        )
        return 0

    lax.fori_loop(1, COLS, greet_col, 0)
    lax.fori_loop(1, ROWS, greet_row, 0)
    pl.semaphore_signal(barrier, inc=1, device_id=(1 - g, row, col), device_id_type=MESH)

    loads = [
        pltpu.make_async_copy(src, dst, in_sems.at[i])
        for i, (src, dst) in enumerate(
            (
                (assignment_in, assignment),
                (steering_in, steering),
                (window_in, window),
                (raw_in, raw),
                (beam_map_in, beam_map),
                (interp_index_in, interp_index),
                (phase_offset_in, phase_offset),
                (phase_rate_in, phase_rate),
                (bank_in, bank),
            )
        )
    ]
    for load in loads:
        load.start()

    steps = (iota((8, 256), 0) * iota((8, 256), 1)).astype(F32) * (1.0 / NS)
    tc, ts = cos_sin(steps)
    twiddle[0] = tc
    twiddle[1] = ts
    sample = iota((256, 128), 0).astype(F32)
    lane = iota((1, 128), 1)
    for m in range(CHUNKS):
        d = ((lane >> 4) * 32 + (16 * m) + (lane & 15)).astype(F32) * (1.0 / 256)
        c, s = cos_sin(sample * d)
        c, s = c.astype(BF16), s.astype(BF16)
        table[m, :256, :128] = c
        table[m, :256, 128:] = -s
        table[m, 256:, :128] = s
        table[m, 256:, 128:] = c

    loads[0].wait()
    own_row = assignment[...].astype(F32)
    eye = iota((P_DEV, P_DEV), 0) == iota((P_DEV, P_DEV), 1)
    before = iota((P_DEV, P_DEV), 1) < iota((P_DEV, P_DEV), 0)
    own_col = jnp.sum(jnp.where(eye, own_row, 0.0), axis=1, keepdims=True)
    rank = jnp.sum(
        jnp.where(before & (own_col == own_row), 1.0, 0.0), axis=1, keepdims=True
    )
    code_col = own_col * SLOTS + rank + (col * CAP).astype(F32)
    place = iota((P_DEV, 128), 0) + 32 * (col % 4)
    code = jnp.sum(
        jnp.where(iota((P_DEV, 128), 1) == place, code_col, 0.0), axis=0, keepdims=True
    )
    code_own[...] = code

    loads[1].wait()
    pick = iota((2 * P_DEV, 2 * P_DEV), 0)
    pick = (pick % P_DEV) * 2 + pick // P_DEV == iota((2 * P_DEV, 2 * P_DEV), 1)
    parts = dot(pick.astype(F32).astype(BF16), steering[...]).astype(BF16)
    st_own[0] = parts[:P_DEV]
    st_own[1] = parts[P_DEV:]

    pl.semaphore_wait(barrier, COLS - 1 + ROWS - 1 + 1)

    parity = col % 2
    first_sends = []
    mine = pl.ds(pl.multiple_of(col * P_DEV, P_DEV), P_DEV)
    for i in (4, 3, 5, 2, 6, 1, 7):
        dest = (col + i) % COLS
        c1 = remote(
            code_own, code_all.at[col], code_send.at[i], code_recv.at[col], (g, row, dest)
        )
        c1.start()
        first_sends.append(c1)
    for i in (4, 3, 5, 2, 6, 1, 7):
        dest = (col + i) % COLS
        c1 = remote(
            st_own.at[dest % 2], st_all.at[mine], st_send.at[i], st_recv.at[col], (g, row, dest)
        )
        c1.start()
        first_sends.append(c1)
    code_all[col] = code_own[...]
    st_all[pl.ds(pl.multiple_of(col * P_DEV, P_DEV), P_DEV), :] = st_own[parity]

    loads[2].wait()
    loads[3].wait()
    scale = 1.0 / math.sqrt(NS)
    for lh in range(2):
        lanes = [pl.ds(256 * t + 128 * lh, 128) for t in range(8)]
        taper = [window[:, lanes[t]] * scale for t in range(8)]
        for pg in range(P_DEV // 16):
            rows = pl.ds(16 * pg, 16)
            xr = [raw[0, rows, lanes[t]].astype(F32) * taper[t] for t in range(8)]
            xi = [raw[1, rows, lanes[t]].astype(F32) * taper[t] for t in range(8)]
            yr, yi = dft8(xr, xi)
            for c in range(8):
                zr, zi = yr[c], yi[c]
                if c:
                    wc = twiddle[0, c : c + 1, 128 * lh : 128 * lh + 128]
                    ws = twiddle[1, c : c + 1, 128 * lh : 128 * lh + 128]
                    zr, zi = zr * wc + zi * ws, zi * wc - zr * ws
                to = pl.ds(P_DEV * c + 16 * pg, 16)
                ybuf[to, 128 * lh : 128 * lh + 128] = zr.astype(BF16)
                ybuf[to, 256 + 128 * lh : 256 + 128 * lh + 128] = zi.astype(BF16)

    z_sends = []
    for m in range(CHUNKS):
        spectrum = dot(ybuf[...], table[m])
        for part in range(2):
            tiles = swap_groups(
                [
                    spectrum[P_DEV * c : P_DEV * c + P_DEV, 128 * part : 128 * part + 128]
                    for c in range(8)
                ]
            )
            for c in range(8):
                dsend[m, c, :, 128 * part : 128 * part + 128] = tiles[c].astype(BF16)

    def to_cols(m):
        mine = pl.ds(pl.multiple_of(col * P_DEV, P_DEV), P_DEV)
        for i in (1, 4, 7, 3, 5, 2, 6):
            dest = (col + i) % COLS
            c1 = remote(
                dsend.at[m, dest],
                zall.at[m, mine],
                z_send.at[m, i],
                z_recv.at[m, col],
                (g, row, dest),
            )
            c1.start()
            z_sends.append(c1)
        zall[m, mine, :] = dsend[m, col]

    to_cols(0)
    to_cols(1)

    def from_cols(wait):
        for i in range(1, COLS):
            wait((col + i) % COLS)

    def wait_code(source):
        remote(
            code_own, code_all.at[source], code_send.at[0], code_recv.at[source], (g, row, source)
        ).wait_recv()

    def wait_steering(source):
        at = pl.ds(pl.multiple_of(source * P_DEV, P_DEV), P_DEV)
        remote(
            st_own.at[0], st_all.at[at], st_send.at[0], st_recv.at[source], (g, row, source)
        ).wait_recv()

    from_cols(wait_code)
    low = code_all[0] + code_all[1] + code_all[2] + code_all[3]
    high = code_all[4] + code_all[5] + code_all[6] + code_all[7]
    codes = jnp.concatenate([low, high], axis=1).astype(I32)
    for y in range(4):
        sel[192 * y : 192 * y + 192] = jnp.where(
            iota((192, 256), 0) + 192 * y == codes, 1.0, 0.0
        ).astype(BF16)
    from_cols(wait_steering)

    row_sends = []

    def to_owners(kind, data, packed, landed):
        mine = pl.ds(pl.multiple_of(row * SLOTS, SLOTS), SLOTS)
        for dy in (2, 1, 3, 0):
            y = (ry + dy) % 4
            block = pl.ds(pl.multiple_of(y * 4 * SLOTS, 4 * SLOTS), 4 * SLOTS)
            packed[block, :] = dot(sel[block, :], data[...]).astype(BF16)
            for dx in (0, 2, 1, 3):
                dest = y * 4 + (rx + dx) % 4
                there = pl.ds(pl.multiple_of(dest * SLOTS, SLOTS), SLOTS)
                if dy == 0 and dx == 0:
                    landed[mine, :] = packed[mine, :]
                    continue
                c1 = remote(
                    packed.at[there],
                    landed.at[mine],
                    r_send.at[kind, 4 * dy + dx],
                    r_recv.at[kind, row],
                    (g, dest, col),
                )
                c1.start()
                row_sends.append(c1)

    def from_rows(kind, packed, landed, dys=(2, 1, 3, 0)):
        for dy in dys:
            for dx in (0, 2, 1, 3):
                if dy == 0 and dx == 0:
                    continue
                source = (ry - dy + 4) % 4 * 4 + (rx - dx + 4) % 4
                at = pl.ds(pl.multiple_of(source * SLOTS, SLOTS), SLOTS)
                remote(
                    packed.at[at],
                    landed.at[at],
                    r_send.at[kind, 0],
                    r_recv.at[kind, source],
                    (g, source, col),
                ).wait_recv()

    def col_pass(i, part):
        return remote(
            w_got.at[part],
            w_got.at[part],
            p_send.at[i],
            p_recv.at[i],
            (g, row, col + 1 - 2 * parity),
        )

    to_owners(2, st_all, w_slots, w_got.at[parity])

    for m in range(CHUNKS):

        def wait_z(source):
            at = pl.ds(pl.multiple_of(source * P_DEV, P_DEV), P_DEV)
            remote(
                dsend.at[m, 0],
                zall.at[m, at],
                z_send.at[m, 0],
                z_recv.at[m, source],
                (g, row, source),
            ).wait_recv()

        from_cols(wait_z)
        to_owners(m, zall.at[m], slots.at[m], got.at[m])

    from_rows(2, w_slots, w_got.at[parity])
    c1 = col_pass(0, parity)
    c1.start()
    row_sends.append(c1)

    for load in loads[4:]:
        load.wait()
    par[...] = jnp.zeros_like(par)
    par[0:4, :] = (interp_index[...] * HALF + beam_map[...]).astype(F32)
    par[8:12, :] = phase_offset[...]
    par[16:20, :] = phase_rate[...]
    columns = par[...].T
    bins = (col * 256 + iota((1, 256), 1)).astype(F32) * (1.0 / NS)
    for ls in range(4):
        code = columns[:, ls : ls + 1].astype(I32)
        picks[ls] = jnp.where(iota((BEAMS, Q * HALF), 1) == code, 1.0, 0.0).astype(BF16)
        angle = columns[:, 8 + ls : 9 + ls] + columns[:, 16 + ls : 17 + ls] * bins
        c, s = cos_sin(angle * (0.5 / math.pi))
        cosb[ls] = c
        sinb[ls] = s
    for q in range(Q):
        bank_nat[:, RT * q : RT * q + RT] = bank[RT * q : RT * q + RT, :]
    lane = iota((RT, RT), 0)
    order = ((lane % 16) * 8 + lane // 16 == iota((RT, RT), 1)).astype(F32).astype(BF16)
    bank_perm[...] = dot(order, bank_nat[...]).astype(BF16)

    weights_t[pl.ds(pl.multiple_of(parity * BEAMS, BEAMS), BEAMS), :] = w_got[parity].T
    col_pass(0, 1 - parity).wait_recv()
    weights_t[pl.ds(pl.multiple_of((1 - parity) * BEAMS, BEAMS), BEAMS), :] = w_got[1 - parity].T

    def half(bit):
        return pl.ds(pl.multiple_of(bit * HALF, HALF), HALF)

    def interpolated(level, m, child_of, matrices, slot):
        both = child[level, m, child_of]
        v = dot(
            jnp.concatenate([both[:, :128], both[:, 128:]], axis=0), matrices[...]
        ).astype(BF16)
        for part in range(2):
            for q in range(Q):
                vbuf[slot, HALF * q : HALF * q + HALF, 128 * part : 128 * part + 128] = v[
                    HALF * part : HALF * part + HALF, RT * q : RT * q + RT
                ]

    def term(level, m, child_of, slot, beams):
        t = dot(picks[2 * level + child_of, beams, :], vbuf[slot])
        tr, ti = t[:, :128], t[:, 128:]
        c = cosb[2 * level + child_of, beams, 128 * m : 128 * m + 128]
        d = sinb[2 * level + child_of, beams, 128 * m : 128 * m + 128]
        return tr * c - ti * d, tr * d + ti * c

    def send(level, m, real, imag, bit, device):
        img[level, m, :, :128] = real.astype(BF16)
        img[level, m, :, 128:] = imag.astype(BF16)
        c1 = remote(
            img.at[level, m],
            child.at[level, m, bit],
            x_send.at[level, m],
            x_recv.at[level, m],
            device,
        )
        c1.start()
        x_sends.append(c1)

    def keep(level, m, real, imag, bit):
        child[level, m, bit, :, :128] = real.astype(BF16)
        child[level, m, bit, :, 128:] = imag.astype(BF16)

    def arrive(level, m, bit, device):
        remote(
            img.at[level, m],
            child.at[level, m, 1 - bit],
            x_send.at[level, m],
            x_recv.at[level, m],
            device,
        ).wait_recv()

    def beams_of(m, bit):
        lhs = jnp.concatenate(
            [weights_t[half(bit), :], weights_t[half(bit + 2), :]], axis=0
        )
        a = dot(lhs, got[m])
        return a[:HALF, :128] - a[HALF:, 128:], a[:HALF, 128:] + a[HALF:, :128]

    sibling = (1 - g, row, col)
    v = row % 2
    partner = (g, row + 1 - 2 * v, col)
    every = slice(None)
    x_sends = []
    for m in range(CHUNKS):
        from_rows(m, slots.at[m], got.at[m])
        send(0, m, *beams_of(m, 1 - g), g, sibling)
        keep(0, m, *beams_of(m, g), g)
        interpolated(0, m, g, bank_perm, 0)
        give_r, give_i = term(0, m, g, 0, half(1 - v))
        keep_r, keep_i = term(0, m, g, 0, half(v))
        arrive(0, m, g, sibling)
        interpolated(0, m, 1 - g, bank_perm, 1)
        r, i = term(0, m, 1 - g, 1, half(1 - v))
        send(1, m, give_r + r, give_i + i, v, partner)
        r, i = term(0, m, 1 - g, 1, half(v))
        keep(1, m, keep_r + r, keep_i + i, v)
    for m in range(CHUNKS):
        interpolated(1, m, v, bank_nat, 0)
        own_r, own_i = term(1, m, v, 0, every)
        arrive(1, m, v, partner)
        interpolated(1, m, 1 - v, bank_nat, 1)
        r, i = term(1, m, 1 - v, 1, every)
        outf[pl.ds(2 * m, BEAMS, stride=4), :] = own_r + r
        outf[pl.ds(2 * m + 1, BEAMS, stride=4), :] = own_i + i
    out[...] = outf[...].astype(BF16)

    for c1 in first_sends + z_sends + row_sends + x_sends:
        c1.wait_send()


def body(
    raw_samples,
    window,
    steering,
    assignment,
    beam_map,
    interp_index,
    phase_offset,
    phase_rate,
    interp_bank,
):
    dma = pltpu.SemaphoreType.DMA
    vmem = pltpu.VMEM
    out = pl.pallas_call(
        kernel,
        out_shape=pltpu.VMEM((4 * BEAMS, 128), BF16),
        in_specs=[pl.BlockSpec(memory_space=pltpu.HBM)] * 9,
        out_specs=pl.BlockSpec(memory_space=pltpu.VMEM),
        scratch_shapes=[
            vmem((2, P_DEV, NS), BF16),
            vmem((1, NS), F32),
            vmem((2 * P_DEV, BEAMS), BF16),
            vmem((1, P_DEV), I32),
            vmem((4, BEAMS), I32),
            vmem((4, BEAMS), I32),
            vmem((4, BEAMS), F32),
            vmem((4, BEAMS), F32),
            vmem((Q * RT, RT), BF16),
            vmem((8 * P_DEV, 512), BF16),
            vmem((CHUNKS, 512, 256), BF16),
            vmem((2, 8, 256), F32),
            vmem((2, P_DEV, BEAMS), BF16),
            vmem((COLS * P_DEV, BEAMS), BF16),
            vmem((1, 128), F32),
            vmem((COLS, 1, 128), F32),
            vmem((CHUNKS, COLS, P_DEV, 256), BF16),
            vmem((CHUNKS, COLS * P_DEV, 256), BF16),
            vmem((ROWS * SLOTS, 256), BF16),
            vmem((CHUNKS, ROWS * SLOTS, 256), BF16),
            vmem((CHUNKS, ROWS * SLOTS, 256), BF16),
            vmem((ROWS * SLOTS, BEAMS), BF16),
            vmem((2, ROWS * SLOTS, BEAMS), BF16),
            vmem((256, ROWS * SLOTS), BF16),
            vmem((128, 128), F32),
            vmem((RT, Q * RT), BF16),
            vmem((RT, Q * RT), BF16),
            vmem((4, BEAMS, Q * HALF), BF16),
            vmem((4, BEAMS, 256), F32),
            vmem((4, BEAMS, 256), F32),
            vmem((2, CHUNKS, HALF, 256), BF16),
            vmem((2, CHUNKS, 2, HALF, 256), BF16),
            vmem((2, Q * HALF, 256), BF16),
            vmem((4 * BEAMS, 128), F32),
            dma((9,)),
            dma((COLS,)),
            dma((COLS,)),
            dma((COLS,)),
            dma((COLS,)),
            dma((CHUNKS, COLS)),
            dma((CHUNKS, COLS)),
            dma((3, ROWS)),
            dma((3, ROWS)),
            dma((4,)),
            dma((4,)),
            dma((2, CHUNKS)),
            dma((2, CHUNKS)),
        ],
        compiler_params=pltpu.CompilerParams(
            collective_id=0, has_side_effects=True, vmem_limit_bytes=56 << 20
        ),
        name="backprojection",
    )(
        raw_samples,
        window.reshape(1, NS),
        steering.reshape(2 * P_DEV, BEAMS),
        assignment.reshape(1, P_DEV),
        beam_map.reshape(4, BEAMS),
        interp_index.reshape(4, BEAMS),
        phase_offset.reshape(4, BEAMS),
        phase_rate.reshape(4, BEAMS),
        interp_bank.reshape(Q * RT, RT),
    )
    out = out.reshape(BEAMS, CHUNKS, 2, RT).transpose(0, 2, 1, 3)
    return out.reshape(1, 1, BEAMS, 2, CHUNKS * RT)


def solution(mesh):
    in_specs = (
        P(None, ("grp", "row", "col"), None),
        P(),
        P(("grp", "row", "col"), None, None),
        P(("grp", "row", "col"), None),
        P(None, "grp", "row", None, None),
        P(None, "grp", "row", None, None),
        P(None, "grp", "row", None, None),
        P(None, "grp", "row", None, None),
        P(),
    )
    out_specs = P("grp", "row", None, None, "col")
    return jax.shard_map(body, mesh=mesh, in_specs=in_specs, out_specs=out_specs, check_vma=False)
```

```python
import math

import jax
import jax.numpy as jnp
from jax import lax
from jax.experimental import pallas as pl
from jax.experimental.pallas import tpu as pltpu
from jax.sharding import PartitionSpec as P

MESH = pl.DeviceIdType.MESH
F32, BF16, I32 = jnp.float32, jnp.bfloat16, jnp.int32

NS = 2048
BEAMS = 128
RT = 128
Q = 8
P_DEV = 32
CAP = 6
ROWS = 16
COLS = 8
SLOTS = COLS * CAP
HALF = BEAMS // 2
CHUNKS = 2

COS = (
    0.9999999890590227,
    -19.73920449945391,
    64.93911745989556,
    -85.45013953088247,
    60.16763095094928,
    -25.967599248494622,
    6.528658161366808,
)
SIN = (
    6.283185302511503,
    -41.341700405317496,
    81.60513138579344,
    -76.70301535379849,
    42.025926985567956,
    -14.89984666736486,
    3.238137509743233,
)


def horner(coefs, y):
    total = jnp.full_like(y, coefs[-1])
    for c in coefs[-2::-1]:
        total = total * y + c
    return total


def cos_sin(turns):
    r = turns - jnp.floor(turns + 0.5)
    y = r * r
    return horner(COS, y), horner(SIN, y) * r


def dft8(xr, xi):
    h = math.sqrt(0.5)
    ur = [xr[j] + xr[j + 4] for j in range(4)]
    ui = [xi[j] + xi[j + 4] for j in range(4)]
    vr = [xr[j] - xr[j + 4] for j in range(4)]
    vi = [xi[j] - xi[j + 4] for j in range(4)]
    wr = [vr[0], (vr[1] + vi[1]) * h, vi[2], (vi[3] - vr[3]) * h]
    wi = [vi[0], (vi[1] - vr[1]) * h, -vr[2], (-vr[3] - vi[3]) * h]
    yr, yi = [None] * 8, [None] * 8
    for odd, (zr, zi) in enumerate(((ur, ui), (wr, wi))):
        ar, ai = zr[0] + zr[2], zi[0] + zi[2]
        br, bi = zr[0] - zr[2], zi[0] - zi[2]
        cr, ci = zr[1] + zr[3], zi[1] + zi[3]
        dr, di = zr[1] - zr[3], zi[1] - zi[3]
        yr[odd], yi[odd] = ar + cr, ai + ci
        yr[odd + 4], yi[odd + 4] = ar - cr, ai - ci
        yr[odd + 2], yi[odd + 2] = br + di, bi - dr
        yr[odd + 6], yi[odd + 6] = br - di, bi + dr
    return yr, yi


def swap_groups(tiles):
    lane = lax.broadcasted_iota(I32, tiles[0].shape, 1)
    tiles = list(tiles)
    for bit in range(3):
        step = 1 << bit
        upper = (lane & (16 * step)) != 0
        for a in range(8):
            if a & step:
                continue
            low, high = tiles[a], tiles[a + step]
            tiles[a] = jnp.where(upper, pltpu.roll(high, 16 * step, 1), low)
            tiles[a + step] = jnp.where(upper, high, pltpu.roll(low, 128 - 16 * step, 1))
    return tiles


def dot(a, b):
    return jnp.dot(a, b, preferred_element_type=F32)


def iota(shape, dim):
    return lax.broadcasted_iota(I32, shape, dim)


def kernel(
    raw_in,
    window_in,
    steering_in,
    assignment_in,
    beam_map_in,
    interp_index_in,
    phase_offset_in,
    phase_rate_in,
    bank_in,
    out,
    raw,
    window,
    steering,
    assignment,
    beam_map,
    interp_index,
    phase_offset,
    phase_rate,
    bank,
    ybuf,
    table,
    twiddle,
    st_own,
    st_all,
    code_own,
    code_all,
    dsend,
    zall,
    sel,
    slots,
    got,
    w_slots,
    w_got,
    weights_t,
    par,
    bank_nat,
    bank_perm,
    picks,
    cosb,
    sinb,
    img,
    child,
    vbuf,
    outf,
    in_sems,
    st_send,
    st_recv,
    code_send,
    code_recv,
    z_send,
    z_recv,
    r_send,
    r_recv,
    p_send,
    p_recv,
    x_send,
    x_recv,
):
    g, row, col = lax.axis_index("grp"), lax.axis_index("row"), lax.axis_index("col")
    ry, rx = row // 4, row % 4

    def remote(src, dst, ssem, rsem, device):
        return pltpu.make_async_remote_copy(
            src_ref=src,
            dst_ref=dst,
            send_sem=ssem,
            recv_sem=rsem,
            device_id=device,
            device_id_type=MESH,
        )

    barrier = pltpu.get_barrier_semaphore()

    for i in (4, 3, 5, 2, 6, 1, 7):
        pl.semaphore_signal(
            barrier, inc=1, device_id=(g, row, (col + i) % COLS), device_id_type=MESH
        )

    def greet_row(i, _):
        pl.semaphore_signal(
            barrier, inc=1, device_id=(g, (row + i) % ROWS, col), device_id_type=MESH
        )
        return 0

    lax.fori_loop(1, ROWS, greet_row, 0)
    pl.semaphore_signal(barrier, inc=1, device_id=(1 - g, row, col), device_id_type=MESH)

    loads = [
        pltpu.make_async_copy(src, dst, in_sems.at[i])
        for i, (src, dst) in enumerate(
            (
                (assignment_in, assignment),
                (steering_in, steering),
                (window_in, window),
                (raw_in, raw),
                (beam_map_in, beam_map),
                (interp_index_in, interp_index),
                (phase_offset_in, phase_offset),
                (phase_rate_in, phase_rate),
                (bank_in, bank),
            )
        )
    ]
    for load in loads:
        load.start()

    steps = (iota((8, 256), 0) * iota((8, 256), 1)).astype(F32) * (1.0 / NS)
    tc, ts = cos_sin(steps)
    twiddle[0] = tc
    twiddle[1] = ts
    sample = iota((256, 128), 0).astype(F32)
    lane = iota((1, 128), 1)
    for m in range(CHUNKS):
        d = ((lane >> 4) * 32 + (16 * m) + (lane & 15)).astype(F32) * (1.0 / 256)
        c, s = cos_sin(sample * d)
        c, s = c.astype(BF16), s.astype(BF16)
        table[m, :256, :128] = c
        table[m, :256, 128:] = -s
        table[m, 256:, :128] = s
        table[m, 256:, 128:] = c

    loads[0].wait()
    own_row = assignment[...].astype(F32)
    eye = iota((P_DEV, P_DEV), 0) == iota((P_DEV, P_DEV), 1)
    before = iota((P_DEV, P_DEV), 1) < iota((P_DEV, P_DEV), 0)
    own_col = jnp.sum(jnp.where(eye, own_row, 0.0), axis=1, keepdims=True)
    rank = jnp.sum(
        jnp.where(before & (own_col == own_row), 1.0, 0.0), axis=1, keepdims=True
    )
    code_col = own_col * SLOTS + rank + (col * CAP).astype(F32)
    place = iota((P_DEV, 128), 0) + 32 * (col % 4)
    code = jnp.sum(
        jnp.where(iota((P_DEV, 128), 1) == place, code_col, 0.0), axis=0, keepdims=True
    )
    code_own[...] = code

    loads[1].wait()
    pick = iota((2 * P_DEV, 2 * P_DEV), 0)
    pick = (pick % P_DEV) * 2 + pick // P_DEV == iota((2 * P_DEV, 2 * P_DEV), 1)
    parts = dot(pick.astype(F32).astype(BF16), steering[...]).astype(BF16)
    st_own[0] = parts[:P_DEV]
    st_own[1] = parts[P_DEV:]

    pl.semaphore_wait(barrier, COLS - 1 + ROWS - 1 + 1)

    parity = col % 2
    first_sends = []
    mine = pl.ds(pl.multiple_of(col * P_DEV, P_DEV), P_DEV)
    for i in (4, 3, 5, 2, 6, 1, 7):
        dest = (col + i) % COLS
        c1 = remote(
            code_own, code_all.at[col], code_send.at[i], code_recv.at[col], (g, row, dest)
        )
        c1.start()
        first_sends.append(c1)
    for i in (4, 3, 5, 2, 6, 1, 7):
        dest = (col + i) % COLS
        c1 = remote(
            st_own.at[dest % 2], st_all.at[mine], st_send.at[i], st_recv.at[col], (g, row, dest)
        )
        c1.start()
        first_sends.append(c1)
    code_all[col] = code_own[...]
    st_all[pl.ds(pl.multiple_of(col * P_DEV, P_DEV), P_DEV), :] = st_own[parity]

    loads[2].wait()
    loads[3].wait()
    scale = 1.0 / math.sqrt(NS)
    for lh in range(2):
        lanes = [pl.ds(256 * t + 128 * lh, 128) for t in range(8)]
        taper = [window[:, lanes[t]] * scale for t in range(8)]
        for pg in range(P_DEV // 16):
            rows = pl.ds(16 * pg, 16)
            xr = [raw[0, rows, lanes[t]].astype(F32) * taper[t] for t in range(8)]
            xi = [raw[1, rows, lanes[t]].astype(F32) * taper[t] for t in range(8)]
            yr, yi = dft8(xr, xi)
            for c in range(8):
                zr, zi = yr[c], yi[c]
                if c:
                    wc = twiddle[0, c : c + 1, 128 * lh : 128 * lh + 128]
                    ws = twiddle[1, c : c + 1, 128 * lh : 128 * lh + 128]
                    zr, zi = zr * wc + zi * ws, zi * wc - zr * ws
                to = pl.ds(P_DEV * c + 16 * pg, 16)
                ybuf[to, 128 * lh : 128 * lh + 128] = zr.astype(BF16)
                ybuf[to, 256 + 128 * lh : 256 + 128 * lh + 128] = zi.astype(BF16)

    z_sends = []
    for m in range(CHUNKS):
        spectrum = dot(ybuf[...], table[m])
        for part in range(2):
            tiles = swap_groups(
                [
                    spectrum[P_DEV * c : P_DEV * c + P_DEV, 128 * part : 128 * part + 128]
                    for c in range(8)
                ]
            )
            for c in range(8):
                dsend[m, c, :, 128 * part : 128 * part + 128] = tiles[c].astype(BF16)

    def to_cols(m):
        mine = pl.ds(pl.multiple_of(col * P_DEV, P_DEV), P_DEV)
        for i in (1, 4, 7, 3, 5, 2, 6):
            dest = (col + i) % COLS
            c1 = remote(
                dsend.at[m, dest],
                zall.at[m, mine],
                z_send.at[m, i],
                z_recv.at[m, col],
                (g, row, dest),
            )
            c1.start()
            z_sends.append(c1)
        zall[m, mine, :] = dsend[m, col]

    to_cols(0)
    to_cols(1)

    def from_cols(wait):
        for i in range(1, COLS):
            wait((col + i) % COLS)

    def wait_code(source):
        remote(
            code_own, code_all.at[source], code_send.at[0], code_recv.at[source], (g, row, source)
        ).wait_recv()

    def wait_steering(source):
        at = pl.ds(pl.multiple_of(source * P_DEV, P_DEV), P_DEV)
        remote(
            st_own.at[0], st_all.at[at], st_send.at[0], st_recv.at[source], (g, row, source)
        ).wait_recv()

    from_cols(wait_code)
    low = code_all[0] + code_all[1] + code_all[2] + code_all[3]
    high = code_all[4] + code_all[5] + code_all[6] + code_all[7]
    codes = jnp.concatenate([low, high], axis=1).astype(I32)
    for y in range(4):
        sel[192 * y : 192 * y + 192] = jnp.where(
            iota((192, 256), 0) + 192 * y == codes, 1.0, 0.0
        ).astype(BF16)
    from_cols(wait_steering)

    row_sends = []

    def to_owners(kind, data, packed, landed):
        mine = pl.ds(pl.multiple_of(row * SLOTS, SLOTS), SLOTS)
        for dy in (2, 1, 3, 0):
            y = (ry + dy) % 4
            block = pl.ds(pl.multiple_of(y * 4 * SLOTS, 4 * SLOTS), 4 * SLOTS)
            packed[block, :] = dot(sel[block, :], data[...]).astype(BF16)
            for dx in (0, 2, 1, 3):
                dest = y * 4 + (rx + dx) % 4
                there = pl.ds(pl.multiple_of(dest * SLOTS, SLOTS), SLOTS)
                if dy == 0 and dx == 0:
                    landed[mine, :] = packed[mine, :]
                    continue
                c1 = remote(
                    packed.at[there],
                    landed.at[mine],
                    r_send.at[kind, 4 * dy + dx],
                    r_recv.at[kind, row],
                    (g, dest, col),
                )
                c1.start()
                row_sends.append(c1)

    def from_rows(kind, packed, landed, dys=(2, 1, 3, 0)):
        for dy in dys:
            for dx in (0, 2, 1, 3):
                if dy == 0 and dx == 0:
                    continue
                source = (ry - dy + 4) % 4 * 4 + (rx - dx + 4) % 4
                at = pl.ds(pl.multiple_of(source * SLOTS, SLOTS), SLOTS)
                remote(
                    packed.at[at],
                    landed.at[at],
                    r_send.at[kind, 0],
                    r_recv.at[kind, source],
                    (g, source, col),
                ).wait_recv()

    def col_pass(i, part):
        y = (ry - i + 4) % 4
        block = pl.ds(pl.multiple_of(y * 4 * SLOTS, 4 * SLOTS), 4 * SLOTS)
        return remote(
            w_got.at[part, block],
            w_got.at[part, block],
            p_send.at[i],
            p_recv.at[i],
            (g, row, col + 1 - 2 * parity),
        )

    to_owners(2, st_all, w_slots, w_got.at[parity])

    for m in range(CHUNKS):

        def wait_z(source):
            at = pl.ds(pl.multiple_of(source * P_DEV, P_DEV), P_DEV)
            remote(
                dsend.at[m, 0],
                zall.at[m, at],
                z_send.at[m, 0],
                z_recv.at[m, source],
                (g, row, source),
            ).wait_recv()

        from_cols(wait_z)
        to_owners(m, zall.at[m], slots.at[m], got.at[m])

    for dy in (2, 1, 3, 0):
        from_rows(2, w_slots, w_got.at[parity], (dy,))
        c1 = col_pass(dy, parity)
        c1.start()
        row_sends.append(c1)

    for load in loads[4:]:
        load.wait()
    par[...] = jnp.zeros_like(par)
    par[0:4, :] = (interp_index[...] * HALF + beam_map[...]).astype(F32)
    par[8:12, :] = phase_offset[...]
    par[16:20, :] = phase_rate[...]
    columns = par[...].T
    bins = (col * 256 + iota((1, 256), 1)).astype(F32) * (1.0 / NS)
    for ls in range(4):
        code = columns[:, ls : ls + 1].astype(I32)
        picks[ls] = jnp.where(iota((BEAMS, Q * HALF), 1) == code, 1.0, 0.0).astype(BF16)
        angle = columns[:, 8 + ls : 9 + ls] + columns[:, 16 + ls : 17 + ls] * bins
        c, s = cos_sin(angle * (0.5 / math.pi))
        cosb[ls] = c
        sinb[ls] = s
    for q in range(Q):
        bank_nat[:, RT * q : RT * q + RT] = bank[RT * q : RT * q + RT, :]
    lane = iota((RT, RT), 0)
    order = ((lane % 16) * 8 + lane // 16 == iota((RT, RT), 1)).astype(F32).astype(BF16)
    bank_perm[...] = dot(order, bank_nat[...]).astype(BF16)

    weights_t[pl.ds(pl.multiple_of(parity * BEAMS, BEAMS), BEAMS), :] = w_got[parity].T
    for dy in (2, 1, 3, 0):
        col_pass(dy, 1 - parity).wait_recv()
    weights_t[pl.ds(pl.multiple_of((1 - parity) * BEAMS, BEAMS), BEAMS), :] = w_got[1 - parity].T

    def half(bit):
        return pl.ds(pl.multiple_of(bit * HALF, HALF), HALF)

    def interpolated(level, m, child_of, matrices, slot):
        both = child[level, m, child_of]
        v = dot(
            jnp.concatenate([both[:, :128], both[:, 128:]], axis=0), matrices[...]
        ).astype(BF16)
        for part in range(2):
            for q in range(Q):
                vbuf[slot, HALF * q : HALF * q + HALF, 128 * part : 128 * part + 128] = v[
                    HALF * part : HALF * part + HALF, RT * q : RT * q + RT
                ]

    def term(level, m, child_of, slot, beams):
        t = dot(picks[2 * level + child_of, beams, :], vbuf[slot])
        tr, ti = t[:, :128], t[:, 128:]
        c = cosb[2 * level + child_of, beams, 128 * m : 128 * m + 128]
        d = sinb[2 * level + child_of, beams, 128 * m : 128 * m + 128]
        return tr * c - ti * d, tr * d + ti * c

    def send(level, m, real, imag, bit, device):
        img[level, m, :, :128] = real.astype(BF16)
        img[level, m, :, 128:] = imag.astype(BF16)
        c1 = remote(
            img.at[level, m],
            child.at[level, m, bit],
            x_send.at[level, m],
            x_recv.at[level, m],
            device,
        )
        c1.start()
        x_sends.append(c1)

    def keep(level, m, real, imag, bit):
        child[level, m, bit, :, :128] = real.astype(BF16)
        child[level, m, bit, :, 128:] = imag.astype(BF16)

    def arrive(level, m, bit, device):
        remote(
            img.at[level, m],
            child.at[level, m, 1 - bit],
            x_send.at[level, m],
            x_recv.at[level, m],
            device,
        ).wait_recv()

    def beams_of(m, bit):
        lhs = jnp.concatenate(
            [weights_t[half(bit), :], weights_t[half(bit + 2), :]], axis=0
        )
        a = dot(lhs, got[m])
        return a[:HALF, :128] - a[HALF:, 128:], a[:HALF, 128:] + a[HALF:, :128]

    sibling = (1 - g, row, col)
    v = row % 2
    partner = (g, row + 1 - 2 * v, col)
    every = slice(None)
    x_sends = []
    for m in range(CHUNKS):
        from_rows(m, slots.at[m], got.at[m])
        send(0, m, *beams_of(m, 1 - g), g, sibling)
        keep(0, m, *beams_of(m, g), g)
        interpolated(0, m, g, bank_perm, 0)
        give_r, give_i = term(0, m, g, 0, half(1 - v))
        keep_r, keep_i = term(0, m, g, 0, half(v))
        arrive(0, m, g, sibling)
        interpolated(0, m, 1 - g, bank_perm, 1)
        r, i = term(0, m, 1 - g, 1, half(1 - v))
        send(1, m, give_r + r, give_i + i, v, partner)
        r, i = term(0, m, 1 - g, 1, half(v))
        keep(1, m, keep_r + r, keep_i + i, v)
    for m in range(CHUNKS):
        interpolated(1, m, v, bank_nat, 0)
        own_r, own_i = term(1, m, v, 0, every)
        arrive(1, m, v, partner)
        interpolated(1, m, 1 - v, bank_nat, 1)
        r, i = term(1, m, 1 - v, 1, every)
        outf[pl.ds(2 * m, BEAMS, stride=4), :] = own_r + r
        outf[pl.ds(2 * m + 1, BEAMS, stride=4), :] = own_i + i
    out[...] = outf[...].astype(BF16)

    for c1 in first_sends + z_sends + row_sends + x_sends:
        c1.wait_send()


def body(
    raw_samples,
    window,
    steering,
    assignment,
    beam_map,
    interp_index,
    phase_offset,
    phase_rate,
    interp_bank,
):
    dma = pltpu.SemaphoreType.DMA
    vmem = pltpu.VMEM
    out = pl.pallas_call(
        kernel,
        out_shape=pltpu.VMEM((4 * BEAMS, 128), BF16),
        in_specs=[pl.BlockSpec(memory_space=pltpu.HBM)] * 9,
        out_specs=pl.BlockSpec(memory_space=pltpu.VMEM),
        scratch_shapes=[
            vmem((2, P_DEV, NS), BF16),
            vmem((1, NS), F32),
            vmem((2 * P_DEV, BEAMS), BF16),
            vmem((1, P_DEV), I32),
            vmem((4, BEAMS), I32),
            vmem((4, BEAMS), I32),
            vmem((4, BEAMS), F32),
            vmem((4, BEAMS), F32),
            vmem((Q * RT, RT), BF16),
            vmem((8 * P_DEV, 512), BF16),
            vmem((CHUNKS, 512, 256), BF16),
            vmem((2, 8, 256), F32),
            vmem((2, P_DEV, BEAMS), BF16),
            vmem((COLS * P_DEV, BEAMS), BF16),
            vmem((1, 128), F32),
            vmem((COLS, 1, 128), F32),
            vmem((CHUNKS, COLS, P_DEV, 256), BF16),
            vmem((CHUNKS, COLS * P_DEV, 256), BF16),
            vmem((ROWS * SLOTS, 256), BF16),
            vmem((CHUNKS, ROWS * SLOTS, 256), BF16),
            vmem((CHUNKS, ROWS * SLOTS, 256), BF16),
            vmem((ROWS * SLOTS, BEAMS), BF16),
            vmem((2, ROWS * SLOTS, BEAMS), BF16),
            vmem((256, ROWS * SLOTS), BF16),
            vmem((128, 128), F32),
            vmem((RT, Q * RT), BF16),
            vmem((RT, Q * RT), BF16),
            vmem((4, BEAMS, Q * HALF), BF16),
            vmem((4, BEAMS, 256), F32),
            vmem((4, BEAMS, 256), F32),
            vmem((2, CHUNKS, HALF, 256), BF16),
            vmem((2, CHUNKS, 2, HALF, 256), BF16),
            vmem((2, Q * HALF, 256), BF16),
            vmem((4 * BEAMS, 128), F32),
            dma((9,)),
            dma((COLS,)),
            dma((COLS,)),
            dma((COLS,)),
            dma((COLS,)),
            dma((CHUNKS, COLS)),
            dma((CHUNKS, COLS)),
            dma((3, ROWS)),
            dma((3, ROWS)),
            dma((4,)),
            dma((4,)),
            dma((2, CHUNKS)),
            dma((2, CHUNKS)),
        ],
        compiler_params=pltpu.CompilerParams(
            collective_id=0, has_side_effects=True, vmem_limit_bytes=56 << 20
        ),
        name="backprojection",
    )(
        raw_samples,
        window.reshape(1, NS),
        steering.reshape(2 * P_DEV, BEAMS),
        assignment.reshape(1, P_DEV),
        beam_map.reshape(4, BEAMS),
        interp_index.reshape(4, BEAMS),
        phase_offset.reshape(4, BEAMS),
        phase_rate.reshape(4, BEAMS),
        interp_bank.reshape(Q * RT, RT),
    )
    out = out.reshape(BEAMS, CHUNKS, 2, RT).transpose(0, 2, 1, 3)
    return out.reshape(1, 1, BEAMS, 2, CHUNKS * RT)


def solution(mesh):
    in_specs = (
        P(None, ("grp", "row", "col"), None),
        P(),
        P(("grp", "row", "col"), None, None),
        P(("grp", "row", "col"), None),
        P(None, "grp", "row", None, None),
        P(None, "grp", "row", None, None),
        P(None, "grp", "row", None, None),
        P(None, "grp", "row", None, None),
        P(),
    )
    out_specs = P("grp", "row", None, None, "col")
    return jax.shard_map(body, mesh=mesh, in_specs=in_specs, out_specs=out_specs, check_vma=False)
```
